256 devices in a mesh: grp: 4 (over y), wide: 64 (over x, z, core).
Axes of the slice: x: 4, y: 4, z: 8, core: 2. Of those that a mesh axis runs over, the one named last changes fastest.
Arguments:
- word_table: float32 [32768, 500], P('wide'), may hold values from -1.5 to 1.5
- word_accum: float32 [32768], P('wide'), may hold values from 0.5 to 8
- ent_table: float32 [131072, 500], P(('grp', 'wide')), may hold values from -1.5 to 1.5
- ent_accum: float32 [131072], P(('grp', 'wide')), may hold values from 0.5 to 8
- anchor_word_shard: int32 [2, 32768, 1], P(None, ('grp', 'wide')), may hold values from 0 to 63; in each aligned block of 128 rows (0 to 127, 128 to 255, ..., all dimensions but the last counted through in order) at most 4 rows name the same one
- anchor_word_row: int32 [2, 32768], P(None, ('grp', 'wide')), may hold values from 0 to 511
- anchor_ent_row: int32 [2, 32768], P(None, ('grp', 'wide')), may hold values from 0 to 511
- anchor_count: int32 [2, 256], P(None, ('grp', 'wide')), may hold values from 16 to 128
- link_src_row: int32 [2, 32768], P(None, ('grp', 'wide')), may hold values from 0 to 511
- link_dst_shard: int32 [2, 32768, 1], P(None, ('grp', 'wide')), may hold values from 0 to 63; in each aligned block of 128 rows (0 to 127, 128 to 255, ..., all dimensions but the last counted through in order) at most 4 rows name the same one
- link_dst_row: int32 [2, 32768], P(None, ('grp', 'wide')), may hold values from 0 to 511
- link_count: int32 [2, 256], P(None, ('grp', 'wide')), may hold values from 16 to 128
- neg_rows: int32 [2, 512, 512], P(None, ('grp', 'wide')), may hold values from 0 to 511
Outputs:
- word_new: float32 [32768, 500], P('wide')
- word_accum_new: float32 [32768], P('wide')
- ent_new: float32 [131072, 500], P(('grp', 'wide'))
- ent_accum_new: float32 [131072], P(('grp', 'wide'))
The draws below stay inside these ranges and needn't reach their ends.
Inputs may be any that keep to these rules, and one draw needn't show every extreme that they name: `anchor_word_shard`: in each minibatch, the 128 anchor rows of one device name any one shard at most 4 times, a bound that some block reaches. `link_dst_shard`: in each minibatch, the 128 link rows of one device name any one shard at most 4 times, a bound that some block reaches.
All inputs are finite; a program needn't handle non-finite values.
Results may differ from the reference program's by a relative error of at most 0.0017.
Values may be sent and summed in bfloat16 or wider, within the bound.
No kernel may reach another device: no remote copies, remote signals or barrier semaphores. Data moves between devices by JAX's collectives and lax.ppermute only.
A program may use at most 64 MiB of HBM per device.

```python
import math
import jax
import jax.numpy as jnp
import numpy as np
from jax import lax

D = 500
VW_DEV = 512
NE_DEV = 512
BLK = 1
BLOCK = 128
NEG = 512
STEPS = 2
ROWS = 128
CAP = 4
VW = 32768
NE = 131072
TOTAL = 32768
BLOCKS = 256
N_GRP = 4
N_WIDE = 64


def touch_ends(values, rng, least, top_value):
    shape = values.shape
    spot = [jax.random.randint(jax.random.fold_in(rng, axis), (), 0, shape[axis]) for axis in range(len(shape))]
    values = values.at[tuple(spot)].set(least)
    longest = shape.index(max(shape))
    spot[longest] = (spot[longest] + 1) % shape[longest]
    return values.at[tuple(spot)].set(top_value)


def level_of(stream_key, dims, shards, smallest, high):
    def one(axis_at, shards_of):
        steps = jax.random.uniform(jax.random.fold_in(jax.random.fold_in(stream_key, 6), axis_at), (shards_of,), jnp.float32, smallest / len(shards), high / len(shards))
        return jnp.repeat(jnp.exp(steps), dims[axis_at] // shards_of).reshape((-1,) + (1,) * (len(dims) - axis_at - 1))

    gain = one(*shards[0])
    for cut in shards[1:]:
        gain = gain * one(*cut)
    return gain


def assign_block(key, own, number, rows, amount, top, limit, slope):
    ranking = jax.random.permutation(key, amount)
    crowded, ordinary = portions_of(amount, rows * top, limit, slope, True), portions_of(amount, rows * top, limit, slope, False)
    places = jnp.arange(amount)

    def named(sizes, rotation):
        used = int((sizes > 0).sum())
        fixed = max(1, used // 4)
        passed = fixed + (places - fixed + rotation * (used - fixed)) % max(1, amount - fixed)
        return jnp.zeros((amount,), jnp.int32).at[ranking[jnp.where(places < fixed, places, passed)]].set(jnp.asarray(sizes, jnp.int32))

    sizes = jnp.where(number % 4 == 0, named(crowded, number // 4), named(ordinary, number - number // 4 - 1))
    mixed = jax.random.permutation(jax.random.fold_in(own, 3), amount)
    source_of, sink = mixed[0:amount // 2 * 2:2], mixed[1:amount // 2 * 2:2]
    room = jnp.minimum(sizes[source_of] - 1, limit - sizes[sink]) // 2
    room = jnp.where((source_of == ranking[0]) | (sink == ranking[0]) | (sizes[sink] == 0), 0, jnp.maximum(room, 0))
    passed = jax.random.randint(jax.random.fold_in(own, 4), (amount // 2,), 0, 1 << 20) % (room + 1)
    sizes = sizes.at[source_of].add(-passed).at[sink].add(passed)
    labels = jnp.searchsorted(jnp.cumsum(sizes), jnp.arange(rows * top), side="right").astype(jnp.int32)
    grid = labels.reshape(top, rows).T
    grid = grid[jax.random.permutation(jax.random.fold_in(own, 1), rows)]
    rotation = jax.random.randint(jax.random.fold_in(own, 2), (rows, 1), 0, top)
    return jnp.take_along_axis(grid, (jnp.arange(top)[None, :] + rotation) % top, axis=1)


def portions_of(number_of, total, limit, slope, full):
    weights = [(1 << 20) // math.isqrt(standing ** slope) + 1 for standing in range(1, number_of + 1)]
    largest = limit if full else min(limit, max(-(-total // number_of), total * weights[0] // sum(weights)))
    least = 1 if total - largest >= number_of - 1 else 0
    counts, rest = [largest] + [least] * (number_of - 1), total - largest - least * (number_of - 1)
    while rest > 0:
        free = [i for i in range(1, number_of) if counts[i] < largest] or [i for i in range(1, number_of) if counts[i] < limit]
        whole, budget = sum([weights[i] for i in free]), rest
        for i in free:
            addition = min(limit - counts[i], max(1, budget * weights[i] // whole), rest)
            counts[i] = counts[i] + addition
            rest = rest - addition
    return np.array(counts)


def gaussian(key, extent, width, most, split=(), kind=jnp.bfloat16):
    factor_of = level_of(key, extent, split, -0.22, 0.18) if split else 1.0
    result = jax.random.normal(key, extent, jnp.float32) * width * factor_of
    return jnp.minimum(jnp.maximum(result, -most), most).astype(kind)


def setup_inputs(seed: int = 0) -> dict:
    key_list = jax.random.split(jax.random.key(seed), 14)
    word_table = gaussian(key_list[0], (VW, D), 0.25, 1.5, ((0, 64),), jnp.float32)
    word_accum = jnp.clip(jnp.exp(math.log(8.0) - 2.7725887 * jax.random.uniform(key_list[1], (VW,), jnp.float32) ** level_of(key_list[1], (VW,), ((0, 64),), -0.2, 0.2)), 0.5, 8.0)
    ent_table = gaussian(key_list[2], (NE, D), 0.25, 1.5, ((0, 256),), jnp.float32)
    ent_accum = jnp.clip(jnp.exp(math.log(8.0) - 2.7725887 * jax.random.uniform(key_list[3], (NE,), jnp.float32) ** level_of(key_list[3], (NE,), ((0, 256),), -0.2, 0.2)), 0.5, 8.0)
    anchor_word_shard_keys = jax.random.split(jax.random.fold_in(key_list[4], 1), STEPS * TOTAL // ROWS)
    anchor_word_shard_turns = jax.random.permutation(jax.random.fold_in(key_list[4], 3), STEPS * TOTAL // ROWS)
    anchor_word_shard = jax.vmap(lambda own, number: assign_block(jax.random.fold_in(key_list[4], 2), own, number, ROWS, N_WIDE, 1, CAP, 2))(anchor_word_shard_keys, anchor_word_shard_turns).reshape((STEPS, TOTAL, 1))
    anchor_word_row = touch_ends(jax.random.randint(key_list[5], (STEPS, TOTAL), 0, VW_DEV), jax.random.fold_in(key_list[5], 1), 0, VW_DEV - 1).astype(jnp.int32)
    anchor_ent_row = touch_ends(jax.random.randint(key_list[6], (STEPS, TOTAL), 0, NE_DEV), jax.random.fold_in(key_list[6], 1), 0, NE_DEV - 1).astype(jnp.int32)
    anchor_count = touch_ends(jax.random.randint(key_list[7], (STEPS, BLOCKS), BLOCK // 8, BLOCK + 1), jax.random.fold_in(key_list[7], 1), BLOCK // 8, BLOCK).astype(jnp.int32)
    link_src_row = touch_ends(jax.random.randint(key_list[8], (STEPS, TOTAL), 0, NE_DEV), jax.random.fold_in(key_list[8], 1), 0, NE_DEV - 1).astype(jnp.int32)
    link_dst_shard_keys = jax.random.split(jax.random.fold_in(key_list[9], 1), STEPS * TOTAL // ROWS)
    link_dst_shard_turns = jax.random.permutation(jax.random.fold_in(key_list[9], 3), STEPS * TOTAL // ROWS)
    link_dst_shard = jax.vmap(lambda own, number: assign_block(jax.random.fold_in(key_list[9], 2), own, number, ROWS, N_WIDE, 1, CAP, 2))(link_dst_shard_keys, link_dst_shard_turns).reshape((STEPS, TOTAL, 1))
    link_dst_row = touch_ends(jax.random.randint(key_list[10], (STEPS, TOTAL), 0, NE_DEV), jax.random.fold_in(key_list[10], 1), 0, NE_DEV - 1).astype(jnp.int32)
    link_count = touch_ends(jax.random.randint(key_list[11], (STEPS, BLOCKS), BLOCK // 8, BLOCK + 1), jax.random.fold_in(key_list[11], 1), BLOCK // 8, BLOCK).astype(jnp.int32)
    neg_rows = touch_ends(jax.random.randint(key_list[12], (STEPS, 2 * BLOCKS, NEG), 0, NE_DEV), jax.random.fold_in(key_list[12], 1), 0, NE_DEV - 1).astype(jnp.int32)
    return {"word_table": word_table, "word_accum": word_accum, "ent_table": ent_table, "ent_accum": ent_accum, "anchor_word_shard": anchor_word_shard, "anchor_word_row": anchor_word_row, "anchor_ent_row": anchor_ent_row, "anchor_count": anchor_count, "link_src_row": link_src_row, "link_dst_shard": link_dst_shard, "link_dst_row": link_dst_row, "link_count": link_count, "neg_rows": neg_rows}


LEARN = 0.1

def block_grads(center_vectors, targets, negative_vectors, valid_mask):
    center_float = center_vectors.astype(jnp.float32)
    target_float = targets.astype(jnp.float32)
    negative_float = negative_vectors.astype(jnp.float32)
    positive = lax.optimization_barrier(jnp.sum(center_float * target_float, axis=-1))
    logit_scores = jnp.einsum('avw,apw->avp', center_float, negative_float)
    attract_factor = valid_mask * (jax.nn.sigmoid(positive) - 1.0)
    repel_factor = (valid_mask[:, :, None] * jax.nn.sigmoid(logit_scores)).astype(jnp.bfloat16)
    repel_float = repel_factor.astype(jnp.float32)
    center_gradient = attract_factor[:, :, None] * target_float + jnp.einsum('sig,sgp->sip', repel_float, negative_float)
    grad_target = attract_factor[:, :, None] * center_float
    negative_gradient = jnp.einsum('urv,urc->uvc', repel_float, center_float)
    return (center_gradient, grad_target, negative_gradient)

def adagrad(embedding, accumulator, gradient):
    accumulator = accumulator + lax.optimization_barrier(jnp.mean(gradient * gradient, axis=1))
    return (embedding - LEARN * gradient / jnp.sqrt(accumulator)[:, None], accumulator)

def reference(word_table, word_accum, ent_table, ent_accum, anchor_word_shard, anchor_word_row, anchor_ent_row, anchor_count, link_src_row, link_dst_shard, link_dst_row, link_count, neg_rows):
    row_count = BLK * BLOCK
    device_count = N_GRP * N_WIDE
    offsets = jnp.arange(BLOCK, dtype=jnp.int32)
    for minibatch in range(STEPS):
        word_half = word_table.astype(jnp.bfloat16)
        ent_half = ent_table.astype(jnp.bfloat16)

        def per_device(totals, device):
            word_grad, ent_grad = totals
            group_index = device // N_WIDE
            first_row = (device * row_count).astype(jnp.int32)

            def device_slice(values):
                return lax.dynamic_slice_in_dim(values, first_row, row_count)
            word_ids = device_slice(anchor_word_shard[minibatch, :, 0]) * VW_DEV + device_slice(anchor_word_row[minibatch])
            own_base = device * NE_DEV
            anchor_ents = own_base + device_slice(anchor_ent_row[minibatch])
            source_ids = own_base + device_slice(link_src_row[minibatch])
            target_ids = (group_index * N_WIDE + device_slice(link_dst_shard[minibatch, :, 0])) * NE_DEV + device_slice(link_dst_row[minibatch])
            negative_vectors = own_base + lax.dynamic_slice_in_dim(neg_rows[minibatch], (device * 2 * BLK).astype(jnp.int32), 2 * BLK)
            anchor_counts = lax.dynamic_slice_in_dim(anchor_count[minibatch], (device * BLK).astype(jnp.int32), BLK)
            link_counts = lax.dynamic_slice_in_dim(link_count[minibatch], (device * BLK).astype(jnp.int32), BLK)
            anchor_mask = (offsets[None, :] < anchor_counts[:, None]).astype(jnp.float32)
            link_mask = (offsets[None, :] < link_counts[:, None]).astype(jnp.float32)
            center_a, target_a, negative_a = block_grads(word_half[word_ids].reshape(BLK, BLOCK, D), ent_half[anchor_ents].reshape(BLK, BLOCK, D), ent_half[negative_vectors[:BLK]], anchor_mask)
            center_l, target_l, negative_l = block_grads(ent_half[source_ids].reshape(BLK, BLOCK, D), ent_half[target_ids].reshape(BLK, BLOCK, D), ent_half[negative_vectors[BLK:]], link_mask)
            word_grad = word_grad.at[word_ids].add(center_a.reshape(row_count, D))
            ent_grad = ent_grad.at[anchor_ents].add(target_a.reshape(row_count, D))
            ent_grad = ent_grad.at[negative_vectors[:BLK].reshape(-1)].add(negative_a.reshape(BLK * NEG, D))
            ent_grad = ent_grad.at[source_ids].add(center_l.reshape(row_count, D))
            ent_grad = ent_grad.at[target_ids].add(target_l.reshape(row_count, D))
            ent_grad = ent_grad.at[negative_vectors[BLK:].reshape(-1)].add(negative_l.reshape(BLK * NEG, D))
            return ((word_grad, ent_grad), None)
        start_totals = (jnp.zeros(word_table.shape, jnp.float32), jnp.zeros(ent_table.shape, jnp.float32))
        (word_grad, ent_grad), unused = lax.scan(per_device, start_totals, jnp.arange(device_count, dtype=jnp.int32))
        word_table, word_accum = adagrad(word_table, word_accum, word_grad)
        ent_table, ent_accum = adagrad(ent_table, ent_accum, ent_grad)
    return (word_table, word_accum, ent_table, ent_accum)
```

```python
import functools

import jax
import jax.numpy as jnp
from jax import lax
from jax.experimental import pallas as pl
from jax.experimental.pallas import tpu as pltpu
from jax.sharding import PartitionSpec as P

BLOCK = 128
STEPS = 2
LEARN = 0.1
CAP = 4
HALF = 256
CUT = 248
PAD = 2 * HALF
ID_HI = 252
ID_LO = 253
F32 = jnp.float32
BF16 = jnp.bfloat16

PLACE_W, PLACE_L, ANCHOR_ENT, LINK_SRC, RANK_W, RANK_L, WORD_ROW, LINK_ROW = range(8)


def iota(shape, dim):
    return lax.broadcasted_iota(jnp.int32, shape, dim).astype(F32)


def nn(a, b):
    return lax.dot_general(a, b, (((1,), (0,)), ((), ())), preferred_element_type=F32)


def nt(a, b):
    return lax.dot_general(a, b, (((1,), (1,)), ((), ())), preferred_element_type=F32)


def hot(condition):
    return jnp.where(condition, 1.0, 0.0).astype(BF16)


def split(x):
    high = x.astype(BF16)
    return high, (x - high.astype(F32)).astype(BF16)


def kernel_call(body, out_shape, name, scratch=(), smem=(), operands=(), flops=0, moved=0):
    in_specs = [
        pl.BlockSpec(memory_space=pltpu.SMEM if i in smem else pltpu.VMEM)
        for i in range(len(operands))
    ]
    out_specs = jax.tree.map(lambda _: pl.BlockSpec(memory_space=pltpu.VMEM), out_shape)
    return pl.pallas_call(
        body,
        out_shape=out_shape,
        in_specs=in_specs,
        out_specs=out_specs,
        scratch_shapes=list(scratch),
        name=name,
        compiler_params=pltpu.CompilerParams(vmem_limit_bytes=40 * 2**20),
        cost_estimate=pl.CostEstimate(flops=flops, bytes_accessed=moved, transcendentals=0),
    )(*operands)


def prepare_body(aws, awr, aer, lsr, lds, ldr, asks_ref, rows_ref, cols_ref, table):
    peers = asks_ref.shape[0]
    table[...] = jnp.zeros_like(table)
    earlier = hot(iota((BLOCK, BLOCK), 0) < iota((BLOCK, BLOCK), 1))
    peer = iota((peers, BLOCK), 0)
    owned = []
    for step in range(STEPS):
        for kind, (shard_ref, row_ref) in enumerate(((aws, awr), (lds, ldr))):
            shard = shard_ref[step : step + 1, :].astype(F32)
            owner = peer == shard
            before = nn(hot(owner), earlier)
            rank = jnp.sum(jnp.where(owner, before, 0.0), axis=0, keepdims=True)
            base = 8 * step
            table[base + PLACE_W + kind : base + PLACE_W + kind + 1, :] = shard * (2 * CAP) + rank
            table[base + RANK_W + kind : base + RANK_W + kind + 1, :] = rank
            table[base + WORD_ROW + kind : base + WORD_ROW + kind + 1, :] = row_ref[
                step : step + 1, :
            ].astype(F32)
            owned.append(hot(owner))
        table[8 * step + ANCHOR_ENT : 8 * step + ANCHOR_ENT + 1, :] = aer[
            step : step + 1, :
        ].astype(F32)
        table[8 * step + LINK_SRC : 8 * step + LINK_SRC + 1, :] = lsr[step : step + 1, :].astype(
            F32
        )
    rows_ref[...] = table[0:16, :]
    cols = jnp.transpose(table[...])
    cols_ref[...] = cols
    lane = iota((BLOCK, BLOCK), 1)
    asks = jnp.zeros((peers, BLOCK), F32)
    for step in range(STEPS):
        for kind in range(2):
            rank = cols[:, 8 * step + RANK_W + kind : 8 * step + RANK_W + kind + 1]
            row = cols[:, 8 * step + WORD_ROW + kind : 8 * step + WORD_ROW + kind + 1]
            high = jnp.floor(row * (1.0 / 16.0))
            place = (2 * step + kind) * CAP + rank
            value = jnp.where(lane == place, high, jnp.where(lane == place + 64.0, row - 16.0 * high, 0.0))
            asks = asks + nn(owned[2 * step + kind], value.astype(BF16))
    asks_ref[...] = asks.astype(jnp.int32)


def to_half(ref, out_ref, scratch):
    scratch[CUT:HALF, :] = jnp.zeros((HALF - CUT, scratch.shape[1]), F32)
    scratch[PAD - 8 : PAD, :] = jnp.zeros((8, scratch.shape[1]), F32)
    scratch[0:CUT, :] = ref[0:CUT, :]
    scratch[HALF : HALF + ref.shape[0] - CUT, :] = ref[CUT:, :]
    out_ref[...] = scratch[...].astype(BF16)


def halves_body(ent_ref, word_ref, neg_ref, ent_out, word_out, counts_out, scratch):
    to_half(ent_ref, ent_out, scratch)
    to_half(word_ref, word_out, scratch)
    entity = iota((ent_ref.shape[1], neg_ref.shape[1]), 0)
    ones = jnp.ones((8, neg_ref.shape[1]), BF16)
    for i in range(2 * STEPS):
        named = hot(entity == neg_ref[i : i + 1, :].astype(F32))
        counts_out[8 * i : 8 * i + 8, :] = nt(ones, named)


def id_column(asks_ref, which):
    peers = asks_ref.shape[0]
    rows = peers * 2 * CAP
    source = hot(
        lax.broadcasted_iota(jnp.int32, (rows, peers), 0) // (2 * CAP)
        == lax.broadcasted_iota(jnp.int32, (rows, peers), 1)
    )
    spread = nn(source, asks_ref[...].astype(BF16))
    lane = lax.broadcasted_iota(jnp.int32, (rows, BLOCK), 1)
    place = which * CAP + lax.broadcasted_iota(jnp.int32, (rows, BLOCK), 0) % CAP
    weight = jnp.where(lane == place, 16.0, jnp.where(lane == place + 64, 1.0, 0.0))
    return jnp.sum(spread * weight, axis=1, keepdims=True)


def first_half(rows):
    return lax.broadcasted_iota(jnp.int32, (rows, HALF), 0) % (2 * CAP) < CAP


def answer(asks_ref, which, half_ref):
    ids = id_column(asks_ref, which)
    rows = ids.shape[0]
    named = hot(iota((rows, half_ref.shape[1]), 1) == ids)
    low = nt(named, half_ref[0:HALF, :])
    high = nt(named, half_ref[HALF:PAD, :])
    return jnp.where(first_half(rows), low, high).astype(BF16)


def respond_body(step, asks_ref, word_half, ent_half, out_ref):
    out_ref[:, 0:HALF] = answer(asks_ref, 2 * step, word_half)
    out_ref[:, HALF:PAD] = answer(asks_ref, 2 * step + 1, ent_half)


def column(cols_ref, step, which):
    return cols_ref[:, 8 * step + which : 8 * step + which + 1]


def valid(count):
    return jnp.where(lax.broadcasted_iota(jnp.int32, (BLOCK, 1), 0) < count, 1.0, 0.0)


def sigmoid(x):
    return jax.nn.sigmoid(x)


def link_local_body(step, link_count, cols_ref, counts_ref, ent_half, src_out, coef_out, grad_out):
    entities = ent_half.shape[1]
    mask = valid(link_count[step])
    source = hot(iota((BLOCK, entities), 1) == column(cols_ref, step, LINK_SRC))
    src = nt(source, ent_half[...]).astype(BF16)
    src_out[...] = src
    push = (mask * sigmoid(nn(src, ent_half[...]))).astype(BF16).astype(F32)
    count = counts_ref[16 * step + 8 : 16 * step + 9, :]
    coef = push * count
    coef_out[...] = coef
    high, low = split(coef)
    grad_out[...] = nt(high, ent_half[...]) + nt(low, ent_half[...])


def take(recv, place):
    rows = recv.shape[0]
    lane = iota((BLOCK, rows), 1)
    return jnp.concatenate([nn(hot(lane == place), recv), nn(hot(lane == place + CAP), recv)], axis=1)


def put(place, low, high, rows):
    row = iota((rows, BLOCK), 0)
    return nn(hot(row == place), low) + nn(hot(row == place + CAP), high)


def blocks_body(
    step,
    anchor_count,
    link_count,
    recv_ref,
    rows_ref,
    cols_ref,
    counts_ref,
    ent_half,
    src_ref,
    link_grad_ref,
    send_ref,
    words_out,
    coef_out,
    link_out,
):
    entities = ent_half.shape[1]
    message_rows = recv_ref.shape[0]
    words = take(recv_ref[:, 0:HALF], column(cols_ref, step, PLACE_W)).astype(BF16)
    words_out[...] = words
    mask = valid(anchor_count[step])
    score = nn(words, ent_half[...])
    target = iota((BLOCK, entities), 1) == column(cols_ref, step, ANCHOR_ENT)
    pos = jnp.sum(jnp.where(target, score, 0.0), axis=1, keepdims=True)
    pull = mask * (sigmoid(pos) - 1.0)
    push = (mask * sigmoid(score)).astype(BF16).astype(F32)
    count = counts_ref[16 * step : 16 * step + 1, :]
    coef = push * count + jnp.where(target, pull, 0.0)
    coef_out[...] = coef
    high, low = split(coef)
    centre = nt(high, ent_half[...]) + nt(low, ent_half[...])
    word_row = column(cols_ref, step, WORD_ROW)
    id_high = jnp.floor(word_row * (1.0 / 16.0))
    lane = lax.broadcasted_iota(jnp.int32, (BLOCK, PAD), 1) % HALF
    centre = jnp.where(lane == ID_HI, id_high, jnp.where(lane == ID_LO, word_row - 16.0 * id_high, centre))
    centre = centre.astype(BF16)
    place = rows_ref[8 * step + PLACE_W : 8 * step + PLACE_W + 1, :]
    send_ref[:, 0:HALF] = put(place, centre[:, 0:HALF], centre[:, HALF:PAD], message_rows).astype(BF16)

    targets = take(recv_ref[:, HALF:PAD], column(cols_ref, step, PLACE_L))
    src = src_ref[...].astype(F32)
    pos = jnp.sum(src * targets, axis=1, keepdims=True)
    pull = valid(link_count[step]) * (sigmoid(pos) - 1.0)
    link_out[...] = pull * targets + link_grad_ref[...]
    grad = (pull * src).astype(BF16)
    place = rows_ref[8 * step + PLACE_L : 8 * step + PLACE_L + 1, :]
    send_ref[:, HALF:PAD] = put(place, grad[:, 0:HALF], grad[:, HALF:PAD], message_rows).astype(BF16)


def ent_local_body(step, words_ref, coef_ref, src_ref, link_coef_ref, link_ref, cols_ref, out_ref):
    entities = out_ref.shape[1]
    words = jnp.transpose(words_ref[...].astype(F32)).astype(BF16)
    high, low = split(coef_ref[...])
    total = nn(words, high) + nn(words, low)
    src = jnp.transpose(src_ref[...].astype(F32)).astype(BF16)
    high, low = split(link_coef_ref[...])
    total = total + nn(src, high) + nn(src, low)
    source = hot(iota((BLOCK, entities), 1) == column(cols_ref, step, LINK_SRC))
    high, low = split(jnp.transpose(link_ref[...]))
    out_ref[...] = total + nn(high, source) + nn(low, source)


def adagrad(table_ref, accum_ref, low, high, table_out, accum_out):
    width = table_ref.shape[0]
    low = low[0:CUT, :]
    high = high[0 : width - CUT, :]
    square = jnp.sum(low * low, axis=0, keepdims=True) + jnp.sum(high * high, axis=0, keepdims=True)
    accum = accum_ref[...] + square * (1.0 / width)
    accum_out[...] = accum
    rate = LEARN * lax.rsqrt(accum)
    table_out[0:CUT, :] = table_ref[0:CUT, :] - low * rate
    table_out[CUT:, :] = table_ref[CUT:, :] - high * rate


def ent_update_body(
    step, last, asks_ref, recv_ref, local_ref, table_ref, accum_ref, table_out, accum_out, *rest
):
    rows = recv_ref.shape[0]
    named = hot(iota((rows, local_ref.shape[1]), 1) == id_column(asks_ref, 2 * step + 1))
    grads = jnp.transpose(recv_ref[:, HALF:PAD].astype(F32))
    lower = lax.broadcasted_iota(jnp.int32, grads.shape, 1) % (2 * CAP) < CAP
    low = nn(jnp.where(lower, grads, 0.0).astype(BF16), named) + local_ref[0:HALF, :]
    high = nn(jnp.where(lower, 0.0, grads).astype(BF16), named) + local_ref[HALF:PAD, :]
    adagrad(table_ref, accum_ref, low, high, table_out, accum_out)
    if not last:
        half_out, scratch = rest
        to_half(table_out, half_out, scratch)


def word_update_body(step, last, recv_ref, table_ref, accum_ref, *rest):
    if last:
        table_out, accum_out = rest
    else:
        asks_ref, ent_half, table_out, accum_out, send_ref, half, scratch = rest
    words = table_ref.shape[1]
    part = 512
    low = jnp.zeros((HALF, words), F32)
    high = jnp.zeros((HALF, words), F32)
    for start in range(0, recv_ref.shape[0], part):
        grads = recv_ref[start : start + part, :].astype(F32)
        lane = lax.broadcasted_iota(jnp.int32, (part, HALF), 1)
        weight = jnp.where(lane == ID_HI, 16.0, jnp.where(lane == ID_LO, 1.0, 0.0))
        ids = jnp.sum(grads * weight, axis=1, keepdims=True)
        named = hot(iota((part, words), 1) == ids)
        grads = jnp.transpose(grads)
        lower = lax.broadcasted_iota(jnp.int32, grads.shape, 1) % (2 * CAP) < CAP
        low = low + nn(jnp.where(lower, grads, 0.0).astype(BF16), named)
        high = high + nn(jnp.where(lower, 0.0, grads).astype(BF16), named)
    adagrad(table_ref, accum_ref, low, high, table_out, accum_out)
    if not last:
        to_half(table_out, half, scratch)
        respond_body(step + 1, asks_ref, half, ent_half, send_ref)


def shape(*dims, dtype=F32):
    return jax.ShapeDtypeStruct(dims, dtype)


def exchange(x, axis, groups):
    return lax.all_to_all(x, axis, split_axis=0, concat_axis=0, tiled=True)


def on_device(
    word_table,
    word_accum,
    ent_table,
    ent_accum,
    anchor_word_shard,
    anchor_word_row,
    anchor_ent_row,
    anchor_count,
    link_src_row,
    link_dst_shard,
    link_dst_row,
    link_count,
    neg_rows,
):
    peers = lax.axis_size("wide")
    groups = lax.axis_size("grp")
    message = peers * 2 * CAP
    word, ent = word_table.T, ent_table.T
    word_sum, ent_sum = word_accum[None, :], ent_accum[None, :]
    width, words = word.shape
    entities = ent.shape[1]
    anchor_count, link_count = anchor_count[:, 0], link_count[:, 0]
    table_scratch = pltpu.VMEM((PAD, entities), F32)

    asks, rows, cols = kernel_call(
        prepare_body,
        (shape(peers, BLOCK, dtype=jnp.int32), shape(16, BLOCK), shape(BLOCK, BLOCK)),
        "prepare",
        scratch=(pltpu.VMEM((BLOCK, BLOCK), F32),),
        operands=(
            anchor_word_shard[:, :, 0],
            anchor_word_row,
            anchor_ent_row,
            link_src_row,
            link_dst_shard[:, :, 0],
            link_dst_row,
        ),
        moved=2**18,
    )
    asked = exchange(asks[:, None, :], "wide", None)[:, 0, :]
    ent_half, word_half, counts = kernel_call(
        halves_body,
        (
            shape(PAD, entities, dtype=BF16),
            shape(PAD, words, dtype=BF16),
            shape(8 * 2 * STEPS, entities),
        ),
        "halves",
        scratch=(table_scratch,),
        operands=(ent, word, neg_rows.reshape(-1, neg_rows.shape[-1])),
        moved=2**23,
    )
    send = kernel_call(
        functools.partial(respond_body, 0),
        shape(message, PAD, dtype=BF16),
        "respond",
        operands=(asked, word_half, ent_half),
        moved=2**22,
    )
    for step in range(STEPS):
        last = step == STEPS - 1
        recv = exchange(send, "wide", None)
        src, link_coef, link_part = kernel_call(
            functools.partial(link_local_body, step),
            (shape(BLOCK, PAD, dtype=BF16), shape(BLOCK, entities), shape(BLOCK, PAD)),
            "link_local",
            smem=(0,),
            operands=(link_count, cols, counts, ent_half),
            moved=2**22,
        )
        grads, anchor_words, anchor_coef, link_grad = kernel_call(
            functools.partial(blocks_body, step),
            (
                shape(message, PAD, dtype=BF16),
                shape(BLOCK, PAD, dtype=BF16),
                shape(BLOCK, entities),
                shape(BLOCK, PAD),
            ),
            "blocks",
            smem=(0, 1),
            operands=(anchor_count, link_count, recv, rows, cols, counts, ent_half, src, link_part),
            moved=2**22,
        )
        received = exchange(grads, "wide", None)
        local = kernel_call(
            functools.partial(ent_local_body, step),
            shape(PAD, entities),
            "ent_local",
            operands=(anchor_words, anchor_coef, src, link_coef, link_grad, cols),
            moved=2**22,
        )
        mine = jnp.broadcast_to(received[None, :, 0:HALF], (groups, message, HALF))
        every = exchange(mine.reshape(groups * message, HALF), "grp", None)
        out = kernel_call(
            functools.partial(ent_update_body, step, last),
            (shape(width, entities), shape(1, entities))
            + (() if last else (shape(PAD, entities, dtype=BF16),)),
            "ent_update",
            scratch=() if last else (table_scratch,),
            operands=(asked, received, local, ent, ent_sum),
            moved=2**22,
        )
        ent, ent_sum = out[0], out[1]
        if last:
            word, word_sum = kernel_call(
                functools.partial(word_update_body, step, True),
                (shape(width, words), shape(1, words)),
                "word_update",
                operands=(every, word, word_sum),
                moved=2**23,
            )
        else:
            ent_half = out[2]
            word, word_sum, send = kernel_call(
                functools.partial(word_update_body, step, False),
                (shape(width, words), shape(1, words), shape(message, PAD, dtype=BF16)),
                "word_update",
                scratch=(pltpu.VMEM((PAD, words), BF16), pltpu.VMEM((PAD, words), F32)),
                operands=(every, word, word_sum, asked, ent_half),
                moved=2**23,
            )
    return (word.T, word_sum[0], ent.T, ent_sum[0])


def solution(mesh):
    in_specs = (
        P("wide", None),
        P("wide"),
        P(("grp", "wide"), None),
        P(("grp", "wide")),
        P(None, ("grp", "wide"), None),
        P(None, ("grp", "wide")),
        P(None, ("grp", "wide")),
        P(None, ("grp", "wide")),
        P(None, ("grp", "wide")),
        P(None, ("grp", "wide"), None),
        P(None, ("grp", "wide")),
        P(None, ("grp", "wide")),
        P(None, ("grp", "wide"), None),
    )
    out_specs = (P("wide", None), P("wide"), P(("grp", "wide"), None), P(("grp", "wide")))
    return jax.shard_map(
        on_device, mesh=mesh, in_specs=in_specs, out_specs=out_specs, check_vma=False
    )
```

```python
import functools

import jax
import jax.numpy as jnp
from jax import lax
from jax.experimental import pallas as pl
from jax.experimental.pallas import tpu as pltpu
from jax.sharding import PartitionSpec as P

BLOCK = 128
STEPS = 2
LEARN = 0.1
CAP = 4
HALF = 256
CUT = 248
PAD = 2 * HALF
ID_HI = 252
ID_LO = 253
F32 = jnp.float32
BF16 = jnp.bfloat16

PLACE_W, PLACE_L, RANK_W, RANK_L, WORD_ROW, LINK_ROW, ANCHOR_ENT, LINK_SRC, MASK_W, MASK_L = range(10)
STRIDE = 16


def iota(shape, dim):
    return lax.broadcasted_iota(jnp.int32, shape, dim).astype(F32)


def nn(a, b):
    return lax.dot_general(a, b, (((1,), (0,)), ((), ())), preferred_element_type=F32)


def nt(a, b):
    return lax.dot_general(a, b, (((1,), (1,)), ((), ())), preferred_element_type=F32)


def hot(condition):
    return jnp.where(condition, 1.0, 0.0).astype(BF16)


def split(x):
    high = x.astype(BF16)
    return high, (x - high.astype(F32)).astype(BF16)


def kernel_call(body, out_shape, name, operands, scratch=(), hbm=(), hbm_out=(), moved=0, pin=False):
    if pin:
        operands = [pltpu.with_memory_space_constraint(x, pltpu.HBM) for x in operands]

    def space(far):
        return pl.BlockSpec(memory_space=pltpu.HBM if far else pltpu.VMEM)

    return pl.pallas_call(
        body,
        out_shape=out_shape,
        in_specs=[space(i in hbm) for i in range(len(operands))],
        out_specs=tuple(space(i in hbm_out) for i in range(len(out_shape))),
        scratch_shapes=list(scratch),
        name=name,
        compiler_params=pltpu.CompilerParams(vmem_limit_bytes=32 * 2**20),
        cost_estimate=pl.CostEstimate(flops=0, bytes_accessed=moved, transcendentals=0),
    )(*operands)


def fetch(sources, targets, sems):
    copies = [
        pltpu.make_async_copy(source, target, sems.at[i])
        for i, (source, target) in enumerate(zip(sources, targets))
    ]
    for copy in copies:
        copy.start()
    for copy in copies:
        copy.wait()


def prepare_body(*refs):
    sources, (asks_ref, rows_ref, cols_ref), (*held, table, sems) = refs[:8], refs[8:11], refs[11:]
    fetch(sources, held, sems)
    aws, lds, awr, ldr, aer, lsr, anchor_count, link_count = held
    peers = asks_ref.shape[0]
    table[...] = jnp.zeros_like(table)
    earlier = hot(iota((BLOCK, BLOCK), 0) < iota((BLOCK, BLOCK), 1))
    peer = iota((peers, BLOCK), 0)
    spot = iota((1, BLOCK), 1)

    def note(step, which, value):
        table[STRIDE * step + which : STRIDE * step + which + 1, :] = value

    kinds = [(step, kind) for step in range(STEPS) for kind in range(2)]
    shards = [(aws, lds)[kind][step : step + 1, :].astype(F32) for step, kind in kinds]
    owners = [peer == shard for shard in shards]
    owned = [hot(owner) for owner in owners]
    before = nn(jnp.concatenate(owned, axis=0), earlier)
    for i, (step, kind) in enumerate(kinds):
        counted = before[i * peers : (i + 1) * peers, :]
        rank = jnp.sum(jnp.where(owners[i], counted, 0.0), axis=0, keepdims=True)
        note(step, PLACE_W + kind, shards[i] * (2 * CAP) + rank)
        note(step, RANK_W + kind, rank)
        note(step, WORD_ROW + kind, (awr, ldr)[kind][step : step + 1, :].astype(F32))
        limit = (anchor_count, link_count)[kind][0:1, step : step + 1].astype(F32)
        note(step, MASK_W + kind, jnp.where(spot < limit, 1.0, 0.0))
    for step in range(STEPS):
        note(step, ANCHOR_ENT, aer[step : step + 1, :].astype(F32))
        note(step, LINK_SRC, lsr[step : step + 1, :].astype(F32))
    rows_ref[...] = table[0 : STEPS * STRIDE, :]
    cols = jnp.transpose(table[...])
    cols_ref[...] = cols
    lane = iota((BLOCK, BLOCK), 1)
    values = []
    for i, (step, kind) in enumerate(kinds):
        base = STRIDE * step + kind
        rank = cols[:, base + RANK_W : base + RANK_W + 1]
        row = cols[:, base + WORD_ROW : base + WORD_ROW + 1]
        high = jnp.floor(row * (1.0 / 16.0))
        place = i * CAP + rank
        value = jnp.where(
            lane == place, high, jnp.where(lane == place + 64.0, row - 16.0 * high, 0.0)
        )
        values.append(value.astype(BF16))
    asks = nn(jnp.concatenate(owned, axis=1), jnp.concatenate(values, axis=0))
    asks_ref[...] = asks.astype(jnp.int32)


def to_half(ref, out_ref, scratch):
    scratch[CUT:HALF, :] = jnp.zeros((HALF - CUT, scratch.shape[1]), F32)
    scratch[PAD - 8 : PAD, :] = jnp.zeros((8, scratch.shape[1]), F32)
    scratch[0:CUT, :] = ref[0:CUT, :]
    scratch[HALF : HALF + ref.shape[0] - CUT, :] = ref[CUT:, :]
    out_ref[...] = scratch[...].astype(BF16)


def halves_body(
    ent_hbm,
    word_hbm,
    neg_hbm,
    ent_sum_hbm,
    word_sum_hbm,
    ent_out,
    word_out,
    counts_out,
    ent_sum_out,
    word_sum_out,
    ent,
    word,
    neg,
    scratch,
    sems,
):
    fetch(
        (neg_hbm, ent_hbm, word_hbm, ent_sum_hbm, word_sum_hbm),
        (neg, ent, word, ent_sum_out, word_sum_out),
        sems,
    )
    to_half(ent, ent_out, scratch)
    to_half(word, word_out, scratch)
    entity = iota((ent.shape[1], neg.shape[-1]), 0)
    ones = jnp.ones((8, neg.shape[-1]), BF16)
    for i in range(2 * STEPS):
        named = hot(entity == neg[i // 2, i % 2 : i % 2 + 1, :].astype(F32))
        counts_out[8 * i : 8 * i + 8, :] = nt(ones, named)


def id_column(asks_ref, which):
    peers = asks_ref.shape[0]
    rows = peers * 2 * CAP
    source = hot(
        lax.broadcasted_iota(jnp.int32, (rows, peers), 0) // (2 * CAP)
        == lax.broadcasted_iota(jnp.int32, (rows, peers), 1)
    )
    spread = nn(source, asks_ref[...].astype(BF16))
    lane = lax.broadcasted_iota(jnp.int32, (rows, BLOCK), 1)
    place = which * CAP + lax.broadcasted_iota(jnp.int32, (rows, BLOCK), 0) % CAP
    weight = jnp.where(lane == place, 16.0, jnp.where(lane == place + 64, 1.0, 0.0))
    return jnp.sum(spread * weight, axis=1, keepdims=True)


def first_half(rows):
    return lax.broadcasted_iota(jnp.int32, (rows, HALF), 0) % (2 * CAP) < CAP


def named_rows(ids, count):
    return hot(iota((ids.shape[0], count), 1) == ids)


def lookup(named, half_ref):
    both = nt(named, half_ref[...])
    return jnp.where(first_half(named.shape[0]), both[:, 0:HALF], both[:, HALF:]).astype(BF16)


def column(cols_ref, step, which):
    return cols_ref[:, STRIDE * step + which : STRIDE * step + which + 1]


def row_of(rows_ref, step, which):
    return rows_ref[STRIDE * step + which : STRIDE * step + which + 1, :]


def sigmoid(x):
    return jax.nn.sigmoid(x)


def product(coef, half_ref):
    high, low = split(coef)
    both = nt(jnp.concatenate([high, low], axis=0), half_ref[...])
    return both[0 : coef.shape[0], :] + both[coef.shape[0] :, :]


def sources(step, cols_ref, ent_half):
    named = hot(iota((BLOCK, ent_half.shape[1]), 1) == column(cols_ref, step, LINK_SRC))
    return named, nt(named, ent_half[...]).astype(BF16)


def link_send(step, asks_ref, rows_ref, cols_ref, ent_half, out_ref, start):
    ids = id_column(asks_ref, 2 * step + 1)
    out_ref[:, start : start + HALF] = lookup(named_rows(ids, ent_half.shape[1]), ent_half)
    place = jnp.where(
        row_of(rows_ref, step, MASK_L) > 0.0, row_of(rows_ref, step, PLACE_L), -float(2 * CAP)
    )
    _, src = sources(step, cols_ref, ent_half)
    out_ref[:, start + HALF : start + PAD] = put(
        place, src[:, 0:HALF], src[:, HALF:PAD], out_ref.shape[0]
    ).astype(BF16)


def respond_body(asks_ref, rows_ref, cols_ref, word_half, ent_half, out_ref):
    named = named_rows(id_column(asks_ref, 0), word_half.shape[1])
    out_ref[:, 0:HALF] = lookup(named, word_half)
    link_send(0, asks_ref, rows_ref, cols_ref, ent_half, out_ref, HALF)


def take(recv, place):
    rows = recv.shape[0]
    lane = iota((2 * BLOCK, rows), 1)
    named = hot(lane == jnp.concatenate([place, place + CAP], axis=0))
    both = nn(named, recv)
    return jnp.concatenate([both[0:BLOCK, :], both[BLOCK:, :]], axis=1)


def put(place, low, high, rows):
    row = iota((rows, 2 * BLOCK), 0)
    named = hot(row == jnp.concatenate([place, place + CAP], axis=1))
    return nn(named, jnp.concatenate([low, high], axis=0))


def anchor_coefficients(step, words, cols_ref, counts_ref, ent_half):
    mask = column(cols_ref, step, MASK_W)
    score = nn(words, ent_half[...])
    target = iota(score.shape, 1) == column(cols_ref, step, ANCHOR_ENT)
    pos = jnp.sum(jnp.where(target, score, 0.0), axis=1, keepdims=True)
    pull = mask * (sigmoid(pos) - 1.0)
    push = (mask * sigmoid(score)).astype(BF16).astype(F32)
    return push * counts_ref[16 * step : 16 * step + 1, :] + jnp.where(target, pull, 0.0)


def anchor_body(step, recv_ref, rows_ref, cols_ref, counts_ref, ent_half, send_ref):
    words = take(recv_ref[:, 0:HALF], column(cols_ref, step, PLACE_W)).astype(BF16)
    centre = product(anchor_coefficients(step, words, cols_ref, counts_ref, ent_half), ent_half)
    word_row = column(cols_ref, step, WORD_ROW)
    id_high = jnp.floor(word_row * (1.0 / 16.0))
    lane = lax.broadcasted_iota(jnp.int32, (BLOCK, PAD), 1) % HALF
    centre = jnp.where(
        lane == ID_HI, id_high, jnp.where(lane == ID_LO, word_row - 16.0 * id_high, centre)
    ).astype(BF16)
    place = row_of(rows_ref, step, PLACE_W)
    send_ref[...] = put(place, centre[:, 0:HALF], centre[:, HALF:PAD], send_ref.shape[0]).astype(BF16)


def adagrad(table_ref, accum, low, high):
    width = table_ref.shape[0]
    low = low[0:CUT, :]
    high = high[0 : width - CUT, :]
    square = jnp.sum(low * low, axis=0, keepdims=True) + jnp.sum(high * high, axis=0, keepdims=True)
    accum = accum + square * (1.0 / width)
    rate = LEARN * lax.rsqrt(accum)
    table_ref[0:CUT, :] = table_ref[0:CUT, :] - low * rate
    table_ref[CUT:, :] = table_ref[CUT:, :] - high * rate
    return accum


def ent_update_body(
    step,
    last,
    link_at,
    asks_ref,
    rows_ref,
    cols_ref,
    counts_ref,
    recv_ref,
    link_recv,
    ent_half,
    table_hbm,
    accum_ref,
    table_out,
    accum_out,
    *rest,
):
    if last:
        table, sems = rest
    else:
        half_out, links_out, table, scratch, sems = rest
    rows = recv_ref.shape[0]
    table_in = pltpu.make_async_copy(table_hbm, table, sems.at[0])
    table_in.start()
    words = take(recv_ref[:, 0:HALF], column(cols_ref, step, PLACE_W)).astype(BF16)
    coef = anchor_coefficients(step, words, cols_ref, counts_ref, ent_half)
    source, src = sources(step, cols_ref, ent_half)
    mask = column(cols_ref, step, MASK_L)
    push = (mask * sigmoid(nn(src, ent_half[...]))).astype(BF16).astype(F32)
    link_coef = push * counts_ref[16 * step + 8 : 16 * step + 9, :]
    targets = take(link_recv[:, link_at : link_at + HALF], column(cols_ref, step, PLACE_L))
    src_float = src.astype(F32)
    pos = jnp.sum(src_float * targets, axis=1, keepdims=True)
    pull = mask * (sigmoid(pos) - 1.0)
    link_grad = pull * targets + product(link_coef, ent_half)
    centres = jnp.concatenate([words.astype(F32), src_float], axis=0)
    centres = jnp.transpose(centres).astype(BF16)
    high, low = split(jnp.concatenate([coef, link_coef], axis=0))
    total = nn(centres, high) + nn(centres, low)
    high, low = split(jnp.transpose(link_grad))
    total = total + nn(high, source) + nn(low, source)
    named = named_rows(id_column(asks_ref, 2 * step + 1), ent_half.shape[1])
    pushed = jnp.transpose(link_recv[:, link_at + HALF :].astype(F32))
    lower = lax.broadcasted_iota(jnp.int32, (1, rows), 1) % (2 * CAP) < CAP
    held = jnp.where(lower, nt(ent_half[0:HALF, :], named), nt(ent_half[HALF:PAD, :], named))
    part = jnp.sum(pushed * held, axis=0, keepdims=True)
    other = jnp.where(lower, jnp.roll(part, -CAP, axis=1), jnp.roll(part, CAP, axis=1))
    grads = (sigmoid(part + other) - 1.0) * pushed
    low = nn(jnp.where(lower, grads, 0.0).astype(BF16), named) + total[0:HALF, :]
    high = nn(jnp.where(lower, 0.0, grads).astype(BF16), named) + total[HALF:PAD, :]
    table_in.wait()
    accum_out[...] = adagrad(table, accum_ref[...], low, high)
    table_done = pltpu.make_async_copy(table, table_out, sems.at[0])
    table_done.start()
    if not last:
        to_half(table, half_out, scratch)
        link_send(step + 1, asks_ref, rows_ref, cols_ref, half_out, links_out, 0)
    table_done.wait()


def compact_body(recv_ref, out_ref):
    rows = recv_ref.shape[0]
    places = out_ref.shape[1]
    grads = jnp.transpose(recv_ref[...].astype(F32)).astype(BF16)
    row = lax.broadcasted_iota(jnp.int32, (rows, places), 0)
    place = lax.broadcasted_iota(jnp.int32, (rows, places), 1)
    place = place // CAP * (2 * CAP) + place % CAP
    low = nn(grads, hot(row == place))
    high = nn(grads, hot(row == place + CAP))
    out_ref[...] = jnp.concatenate([low[0:CUT, :], high], axis=0).astype(BF16)


def word_gradient(recv_ref, count):
    groups, depth, places = recv_ref.shape
    columns = jnp.concatenate([recv_ref[group] for group in range(groups)], axis=1)
    ids = columns[depth - 8 :, :].astype(F32)
    ids = ids[4:5, :] * 16.0 + ids[5:6, :]
    return nt(columns, hot(iota((count, groups * places), 0) == ids))


def word_update_body(
    step,
    asks_ref,
    recv_ref,
    table_hbm,
    accum_ref,
    table_out,
    accum_out,
    send_ref,
    table,
    half,
    scratch,
    sem,
):
    table_in = pltpu.make_async_copy(table_hbm, table, sem)
    table_in.start()
    named = named_rows(id_column(asks_ref, 2 * step + 2), table.shape[1])
    total = word_gradient(recv_ref, table.shape[1])
    table_in.wait()
    accum_out[...] = adagrad(table, accum_ref[...], total[0:CUT, :], total[CUT:, :])
    table_done = pltpu.make_async_copy(table, table_out, sem)
    table_done.start()
    to_half(table, half, scratch)
    send_ref[...] = lookup(named, half)
    table_done.wait()


def word_final_body(recv_ref, table_ref, accum_ref, table_out, accum_out):
    width, words = table_ref.shape
    grad = word_gradient(recv_ref, words)[0:width, :]
    accum = accum_ref[...] + jnp.sum(grad * grad, axis=0, keepdims=True) * (1.0 / width)
    accum_out[...] = accum
    table_out[...] = table_ref[...] - grad * (LEARN * lax.rsqrt(accum))


def shape(*dims, dtype=F32):
    return jax.ShapeDtypeStruct(dims, dtype)


def exchange(x):
    return lax.all_to_all(x, "wide", split_axis=0, concat_axis=0, tiled=True)


def on_device(
    word_table,
    word_accum,
    ent_table,
    ent_accum,
    anchor_word_shard,
    anchor_word_row,
    anchor_ent_row,
    anchor_count,
    link_src_row,
    link_dst_shard,
    link_dst_row,
    link_count,
    neg_rows,
):
    peers = lax.axis_size("wide")
    message = peers * 2 * CAP
    word, ent = word_table.T, ent_table.T
    word_sum, ent_sum = word_accum[None, :], ent_accum[None, :]
    width, words = word.shape
    entities = ent.shape[1]
    indices = (
        anchor_word_shard[:, :, 0],
        link_dst_shard[:, :, 0],
        anchor_word_row,
        link_dst_row,
        anchor_ent_row,
        link_src_row,
        anchor_count.T,
        link_count.T,
    )
    asks, rows, cols = kernel_call(
        prepare_body,
        (shape(peers, BLOCK, dtype=jnp.int32), shape(STEPS * STRIDE, BLOCK), shape(BLOCK, BLOCK)),
        "prepare",
        indices,
        scratch=[pltpu.VMEM(x.shape, jnp.int32) for x in indices]
        + [pltpu.VMEM((BLOCK, BLOCK), F32), pltpu.SemaphoreType.DMA((len(indices),))],
        hbm=range(len(indices)),
        moved=2**18,
        pin=True,
    )
    asked = exchange(asks[:, None, :])[:, 0, :]
    half_shape = shape(PAD, entities, dtype=BF16)
    ent_half, word_half, counts, ent_sum, word_sum = kernel_call(
        halves_body,
        (
            half_shape,
            shape(PAD, words, dtype=BF16),
            shape(8 * 2 * STEPS, entities),
            shape(1, entities),
            shape(1, words),
        ),
        "halves",
        (ent, word, neg_rows, ent_sum, word_sum),
        scratch=(
            pltpu.VMEM(ent.shape, F32),
            pltpu.VMEM(word.shape, F32),
            pltpu.VMEM(neg_rows.shape, jnp.int32),
            pltpu.VMEM((PAD, entities), F32),
            pltpu.SemaphoreType.DMA((5,)),
        ),
        hbm=range(5),
        moved=2**22,
    )
    send_shape = shape(message, 3 * HALF, dtype=BF16)
    links_shape = shape(message, PAD, dtype=BF16)
    (send,) = kernel_call(
        respond_body,
        (send_shape,),
        "respond",
        (asked, rows, cols, word_half, ent_half),
        moved=2**22,
    )
    for step in range(STEPS):
        last = step == STEPS - 1
        recv = exchange(send)
        if step == 0:
            link_recv, link_at = recv, HALF
        (grads,) = kernel_call(
            functools.partial(anchor_body, step),
            (shape(message, HALF, dtype=BF16),),
            "anchor",
            (recv, rows, cols, counts, ent_half),
            moved=2**22,
        )
        received = exchange(grads)
        held = (pltpu.VMEM((width, entities), F32),)
        out = kernel_call(
            functools.partial(ent_update_body, step, last, link_at),
            (shape(width, entities), shape(1, entities)) + (() if last else (half_shape, links_shape)),
            "ent_update",
            (asked, rows, cols, counts, recv, link_recv, ent_half, ent, ent_sum),
            scratch=held
            + (
                ()
                if last
                else (pltpu.VMEM((PAD, entities), F32),)
            )
            + (pltpu.SemaphoreType.DMA((1,)),),
            hbm=(7,),
            hbm_out=(0,),
            moved=2**23,
        )
        ent, ent_sum = out[0], out[1]
        if not last:
            ent_half = out[2]
            received, links = lax.optimization_barrier((received, out[3]))
            link_recv, link_at = exchange(links), 0
        (mine,) = kernel_call(
            compact_body,
            (shape(CUT + HALF, peers * CAP, dtype=BF16),),
            "compact",
            (received,),
            moved=2**20,
        )
        every = lax.all_gather(mine, "grp", axis=0, tiled=False)
        if last:
            word, word_sum = kernel_call(
                word_final_body,
                (shape(width, words), shape(1, words)),
                "word_final",
                (every, word, word_sum),
                moved=2**23,
            )
        else:
            word, word_sum, send = kernel_call(
                functools.partial(word_update_body, step),
                (shape(width, words), shape(1, words), shape(message, HALF, dtype=BF16)),
                "word_update",
                (asked, every, word, word_sum),
                scratch=(
                    pltpu.VMEM((width, words), F32),
                    pltpu.VMEM((PAD, words), BF16),
                    pltpu.VMEM((PAD, words), F32),
                    pltpu.SemaphoreType.DMA,
                ),
                hbm=(2,),
                hbm_out=(0,),
                moved=2**23,
            )
            send, link_recv = lax.optimization_barrier((send, link_recv))
    return (word.T, word_sum[0], ent.T, ent_sum[0])


def solution(mesh):
    in_specs = (
        P("wide", None),
        P("wide"),
        P(("grp", "wide"), None),
        P(("grp", "wide")),
        P(None, ("grp", "wide"), None),
        P(None, ("grp", "wide")),
        P(None, ("grp", "wide")),
        P(None, ("grp", "wide")),
        P(None, ("grp", "wide")),
        P(None, ("grp", "wide"), None),
        P(None, ("grp", "wide")),
        P(None, ("grp", "wide")),
        P(None, ("grp", "wide"), None),
    )
    out_specs = (P("wide", None), P("wide"), P(("grp", "wide"), None), P(("grp", "wide")))
    return jax.shard_map(
        on_device, mesh=mesh, in_specs=in_specs, out_specs=out_specs, check_vma=False
    )
```

```python
import functools

import jax
import jax.numpy as jnp
from jax import lax
from jax.experimental import pallas as pl
from jax.experimental.pallas import tpu as pltpu
from jax.sharding import PartitionSpec as P

BLOCK = 128
STEPS = 2
LEARN = 0.1
CAP = 4
HALF = 256
CUT = 248
PAD = 2 * HALF
ID_HI = 252
ID_LO = 253
F32 = jnp.float32
BF16 = jnp.bfloat16

PLACE_W, PLACE_L, RANK_W, RANK_L, WORD_ROW, LINK_ROW, ANCHOR_ENT, LINK_SRC, MASK_W, MASK_L = range(10)
STRIDE = 16


def iota(shape, dim):
    return lax.broadcasted_iota(jnp.int32, shape, dim).astype(F32)


def nn(a, b):
    return lax.dot_general(a, b, (((1,), (0,)), ((), ())), preferred_element_type=F32)


def nt(a, b):
    return lax.dot_general(a, b, (((1,), (1,)), ((), ())), preferred_element_type=F32)


def hot(condition):
    return jnp.where(condition, 1.0, 0.0).astype(BF16)


def split(x):
    high = x.astype(BF16)
    return high, (x - high.astype(F32)).astype(BF16)


def kernel_call(body, out_shape, name, operands, scratch=(), hbm=(), hbm_out=(), moved=0, pin=False):
    if pin:
        operands = [
            pltpu.with_memory_space_constraint(x, pltpu.HBM) if i in hbm else x
            for i, x in enumerate(operands)
        ]

    def space(far):
        return pl.BlockSpec(memory_space=pltpu.HBM if far else pltpu.VMEM)

    return pl.pallas_call(
        body,
        out_shape=out_shape,
        in_specs=[space(i in hbm) for i in range(len(operands))],
        out_specs=tuple(space(i in hbm_out) for i in range(len(out_shape))),
        scratch_shapes=list(scratch),
        name=name,
        compiler_params=pltpu.CompilerParams(vmem_limit_bytes=32 * 2**20),
        cost_estimate=pl.CostEstimate(flops=0, bytes_accessed=moved, transcendentals=0),
    )(*operands)


def fetch(sources, targets, sems):
    copies = [
        pltpu.make_async_copy(source, target, sems.at[i])
        for i, (source, target) in enumerate(zip(sources, targets))
    ]
    for copy in copies:
        copy.start()
    for copy in copies:
        copy.wait()


def prepare_body(*refs):
    sources, (asks_ref, rows_ref, cols_ref), (*held, table, sems) = refs[:8], refs[8:11], refs[11:]
    fetch(sources, held, sems)
    aws, lds, awr, ldr, aer, lsr, anchor_count, link_count = held
    peers = asks_ref.shape[0]
    table[...] = jnp.zeros_like(table)
    earlier = hot(iota((BLOCK, BLOCK), 0) < iota((BLOCK, BLOCK), 1))
    peer = iota((peers, BLOCK), 0)
    spot = iota((1, BLOCK), 1)

    def note(step, which, value):
        table[STRIDE * step + which : STRIDE * step + which + 1, :] = value

    kinds = [(step, kind) for step in range(STEPS) for kind in range(2)]
    shards = [(aws, lds)[kind][step : step + 1, :].astype(F32) for step, kind in kinds]
    owners = [peer == shard for shard in shards]
    owned = [hot(owner) for owner in owners]
    before = nn(jnp.concatenate(owned, axis=0), earlier)
    for i, (step, kind) in enumerate(kinds):
        counted = before[i * peers : (i + 1) * peers, :]
        rank = jnp.sum(jnp.where(owners[i], counted, 0.0), axis=0, keepdims=True)
        note(step, PLACE_W + kind, shards[i] * (2 * CAP) + rank)
        note(step, RANK_W + kind, rank)
        note(step, WORD_ROW + kind, (awr, ldr)[kind][step : step + 1, :].astype(F32))
        limit = (anchor_count, link_count)[kind][0:1, step : step + 1].astype(F32)
        note(step, MASK_W + kind, jnp.where(spot < limit, 1.0, 0.0))
    for step in range(STEPS):
        note(step, ANCHOR_ENT, aer[step : step + 1, :].astype(F32))
        note(step, LINK_SRC, lsr[step : step + 1, :].astype(F32))
    rows_ref[...] = table[0 : STEPS * STRIDE, :]
    cols = jnp.transpose(table[...])
    cols_ref[...] = cols
    lane = iota((BLOCK, BLOCK), 1)
    values = []
    for i, (step, kind) in enumerate(kinds):
        base = STRIDE * step + kind
        rank = cols[:, base + RANK_W : base + RANK_W + 1]
        row = cols[:, base + WORD_ROW : base + WORD_ROW + 1]
        high = jnp.floor(row * (1.0 / 16.0))
        place = i * CAP + rank
        value = jnp.where(
            lane == place, high, jnp.where(lane == place + 64.0, row - 16.0 * high, 0.0)
        )
        values.append(value.astype(BF16))
    asks = nn(jnp.concatenate(owned, axis=1), jnp.concatenate(values, axis=0))
    asks_ref[...] = asks.astype(jnp.int32)


def to_half(ref, out_ref, scratch):
    scratch[CUT:HALF, :] = jnp.zeros((HALF - CUT, scratch.shape[1]), F32)
    scratch[PAD - 8 : PAD, :] = jnp.zeros((8, scratch.shape[1]), F32)
    scratch[0:CUT, :] = ref[0:CUT, :]
    scratch[HALF : HALF + ref.shape[0] - CUT, :] = ref[CUT:, :]
    out_ref[...] = scratch[...].astype(BF16)


def halves_body(
    ent_hbm,
    word_hbm,
    neg_hbm,
    ent_sum_hbm,
    word_sum_hbm,
    rows_ref,
    cols_ref,
    ent_out,
    word_out,
    pushed_out,
    counts_out,
    ent_sum_out,
    word_sum_out,
    ent,
    word,
    neg,
    scratch,
    sems,
):
    copies = [
        pltpu.make_async_copy(source, target, sems.at[i])
        for i, (source, target) in enumerate(
            (
                (ent_hbm, ent),
                (word_hbm, word),
                (neg_hbm, neg),
                (ent_sum_hbm, ent_sum_out),
                (word_sum_hbm, word_sum_out),
            )
        )
    ]
    for copy in copies:
        copy.start()
    copies[0].wait()
    to_half(ent, ent_out, scratch)
    pushed_out[...] = pushed_sources(0, rows_ref, cols_ref, ent_out, pushed_out.shape[0])
    copies[1].wait()
    to_half(word, word_out, scratch)
    for copy in copies[2:]:
        copy.wait()
    entity = iota((ent.shape[1], neg.shape[-1]), 0)
    ones = jnp.ones((8, neg.shape[-1]), BF16)
    for i in range(2 * STEPS):
        named = hot(entity == neg[i // 2, i % 2 : i % 2 + 1, :].astype(F32))
        counts_out[8 * i : 8 * i + 8, :] = nt(ones, named)


def id_column(asks_ref, which):
    peers = asks_ref.shape[0]
    rows = peers * 2 * CAP
    source = hot(
        lax.broadcasted_iota(jnp.int32, (rows, peers), 0) // (2 * CAP)
        == lax.broadcasted_iota(jnp.int32, (rows, peers), 1)
    )
    spread = nn(source, asks_ref[...].astype(BF16))
    lane = lax.broadcasted_iota(jnp.int32, (rows, BLOCK), 1)
    place = which * CAP + lax.broadcasted_iota(jnp.int32, (rows, BLOCK), 0) % CAP
    weight = jnp.where(lane == place, 16.0, jnp.where(lane == place + 64, 1.0, 0.0))
    return jnp.sum(spread * weight, axis=1, keepdims=True)


def first_half(rows):
    return lax.broadcasted_iota(jnp.int32, (rows, HALF), 0) % (2 * CAP) < CAP


def named_rows(ids, count):
    return hot(iota((ids.shape[0], count), 1) == ids)


def lookup(named, half_ref):
    both = nt(named, half_ref[...])
    return jnp.where(first_half(named.shape[0]), both[:, 0:HALF], both[:, HALF:]).astype(BF16)


def column(cols_ref, step, which):
    return cols_ref[:, STRIDE * step + which : STRIDE * step + which + 1]


def row_of(rows_ref, step, which):
    return rows_ref[STRIDE * step + which : STRIDE * step + which + 1, :]


def sigmoid(x):
    return jax.nn.sigmoid(x)


def product(coef, half_ref):
    high, low = split(coef)
    both = nt(jnp.concatenate([high, low], axis=0), half_ref[...])
    return both[0 : coef.shape[0], :] + both[coef.shape[0] :, :]


def sources(step, cols_ref, ent_half):
    named = hot(iota((BLOCK, ent_half.shape[1]), 1) == column(cols_ref, step, LINK_SRC))
    return named, nt(named, ent_half[...]).astype(BF16)


def pushed_sources(step, rows_ref, cols_ref, ent_half, rows):
    place = jnp.where(
        row_of(rows_ref, step, MASK_L) > 0.0, row_of(rows_ref, step, PLACE_L), -float(2 * CAP)
    )
    _, src = sources(step, cols_ref, ent_half)
    return put(place, src[:, 0:HALF], src[:, HALF:PAD], rows).astype(BF16)


def asked_rows(which, asks_ref, half_ref):
    return lookup(named_rows(id_column(asks_ref, which), half_ref.shape[1]), half_ref)


def respond_body(asks_ref, pushed_ref, word_half, ent_half, out_ref):
    out_ref[:, 0:HALF] = asked_rows(0, asks_ref, word_half)
    out_ref[:, HALF:PAD] = asked_rows(1, asks_ref, ent_half)
    out_ref[:, PAD:] = pushed_ref[...]


def take(recv, place):
    rows = recv.shape[0]
    lane = iota((2 * BLOCK, rows), 1)
    named = hot(lane == jnp.concatenate([place, place + CAP], axis=0))
    both = nn(named, recv)
    return jnp.concatenate([both[0:BLOCK, :], both[BLOCK:, :]], axis=1)


def put(place, low, high, rows):
    row = iota((rows, 2 * BLOCK), 0)
    named = hot(row == jnp.concatenate([place, place + CAP], axis=1))
    return nn(named, jnp.concatenate([low, high], axis=0))


def anchor_coefficients(step, words, cols_ref, counts_ref, ent_half):
    mask = column(cols_ref, step, MASK_W)
    score = nn(words, ent_half[...])
    target = iota(score.shape, 1) == column(cols_ref, step, ANCHOR_ENT)
    pos = jnp.sum(jnp.where(target, score, 0.0), axis=1, keepdims=True)
    pull = mask * (sigmoid(pos) - 1.0)
    push = (mask * sigmoid(score)).astype(BF16).astype(F32)
    return push * counts_ref[16 * step : 16 * step + 1, :] + jnp.where(target, pull, 0.0)


def anchor_body(step, recv_ref, rows_ref, cols_ref, counts_ref, ent_half, send_ref):
    words = take(recv_ref[:, 0:HALF], column(cols_ref, step, PLACE_W)).astype(BF16)
    centre = product(anchor_coefficients(step, words, cols_ref, counts_ref, ent_half), ent_half)
    word_row = column(cols_ref, step, WORD_ROW)
    id_high = jnp.floor(word_row * (1.0 / 16.0))
    lane = lax.broadcasted_iota(jnp.int32, (BLOCK, PAD), 1) % HALF
    centre = jnp.where(
        lane == ID_HI, id_high, jnp.where(lane == ID_LO, word_row - 16.0 * id_high, centre)
    ).astype(BF16)
    place = row_of(rows_ref, step, PLACE_W)
    send_ref[...] = put(place, centre[:, 0:HALF], centre[:, HALF:PAD], send_ref.shape[0]).astype(BF16)


def adagrad(table_ref, accum, low, high):
    width = table_ref.shape[0]
    low = low[0:CUT, :]
    high = high[0 : width - CUT, :]
    square = jnp.sum(low * low, axis=0, keepdims=True) + jnp.sum(high * high, axis=0, keepdims=True)
    accum = accum + square * (1.0 / width)
    rate = LEARN * lax.rsqrt(accum)
    table_ref[0:CUT, :] = table_ref[0:CUT, :] - low * rate
    table_ref[CUT:, :] = table_ref[CUT:, :] - high * rate
    return accum


def ent_update_body(
    step,
    last,
    link_at,
    asks_ref,
    rows_ref,
    cols_ref,
    counts_ref,
    recv_ref,
    link_recv,
    ent_half,
    table_hbm,
    accum_ref,
    table_out,
    accum_out,
    *rest,
):
    if last:
        table, sems = rest
    else:
        half_out, links_out, table, scratch, sems = rest
    rows = recv_ref.shape[0]
    table_in = pltpu.make_async_copy(table_hbm, table, sems.at[0])
    table_in.start()
    words = take(recv_ref[:, 0:HALF], column(cols_ref, step, PLACE_W)).astype(BF16)
    coef = anchor_coefficients(step, words, cols_ref, counts_ref, ent_half)
    source, src = sources(step, cols_ref, ent_half)
    mask = column(cols_ref, step, MASK_L)
    push = (mask * sigmoid(nn(src, ent_half[...]))).astype(BF16).astype(F32)
    link_coef = push * counts_ref[16 * step + 8 : 16 * step + 9, :]
    targets = take(link_recv[:, link_at : link_at + HALF], column(cols_ref, step, PLACE_L))
    src_float = src.astype(F32)
    pos = jnp.sum(src_float * targets, axis=1, keepdims=True)
    pull = mask * (sigmoid(pos) - 1.0)
    link_grad = pull * targets + product(link_coef, ent_half)
    centres = jnp.concatenate([words.astype(F32), src_float], axis=0)
    centres = jnp.transpose(centres).astype(BF16)
    high, low = split(jnp.concatenate([coef, link_coef], axis=0))
    total = nn(centres, high) + nn(centres, low)
    high, low = split(jnp.transpose(link_grad))
    total = total + nn(high, source) + nn(low, source)
    named = named_rows(id_column(asks_ref, 2 * step + 1), ent_half.shape[1])
    pushed = jnp.transpose(link_recv[:, link_at + HALF :].astype(F32))
    lower = lax.broadcasted_iota(jnp.int32, (1, rows), 1) % (2 * CAP) < CAP
    held = jnp.where(lower, nt(ent_half[0:HALF, :], named), nt(ent_half[HALF:PAD, :], named))
    part = jnp.sum(pushed * held, axis=0, keepdims=True)
    other = jnp.where(lower, jnp.roll(part, -CAP, axis=1), jnp.roll(part, CAP, axis=1))
    grads = (sigmoid(part + other) - 1.0) * pushed
    low = nn(jnp.where(lower, grads, 0.0).astype(BF16), named) + total[0:HALF, :]
    high = nn(jnp.where(lower, 0.0, grads).astype(BF16), named) + total[HALF:PAD, :]
    table_in.wait()
    accum_out[...] = adagrad(table, accum_ref[...], low, high)
    table_done = pltpu.make_async_copy(table, table_out, sems.at[0])
    table_done.start()
    if not last:
        to_half(table, half_out, scratch)
        links_out[:, 0:HALF] = asked_rows(2 * step + 3, asks_ref, half_out)
        links_out[:, HALF:] = pushed_sources(step + 1, rows_ref, cols_ref, half_out, rows)
    table_done.wait()


def compact_body(recv_ref, *outs):
    rows = recv_ref.shape[0]
    places = outs[0].shape[1]
    grads = jnp.transpose(recv_ref[...].astype(F32)).astype(BF16)
    row = lax.broadcasted_iota(jnp.int32, (rows, places), 0)
    place = lax.broadcasted_iota(jnp.int32, (rows, places), 1)
    place = place // CAP * (2 * CAP) + place % CAP
    low = nn(grads, hot(row == place))
    high = nn(grads, hot(row == place + CAP))
    columns = jnp.concatenate([low[0:CUT, :], high], axis=0).astype(BF16)
    outs[0][...] = columns
    for i, out in enumerate(outs[1:]):
        half = out.shape[1]
        out[...] = columns[:, i % 2 * half : (i % 2 + 1) * half]


def word_gradient(columns, count):
    depth, places = columns.shape
    ids = columns[depth - 8 :, :].astype(F32)
    ids = ids[4:5, :] * 16.0 + ids[5:6, :]
    return nt(columns, hot(iota((count, places), 0) == ids))


def joined(first_ref, second_ref):
    return jnp.concatenate([first_ref[...], second_ref[...]], axis=1)


def pair_gradient(mine_ref, far_low, far_high, count):
    mine = word_gradient(mine_ref[...], count)
    return mine + word_gradient(joined(far_low, far_high), count)


def word_near_body(before_low, before_high, after_low, after_high, out_ref):
    count = out_ref.shape[1]
    before = word_gradient(joined(before_low, before_high), count)
    out_ref[...] = before + word_gradient(joined(after_low, after_high), count)


def word_update_body(
    step,
    asks_ref,
    mine_ref,
    far_low,
    far_high,
    near_ref,
    table_hbm,
    accum_ref,
    table_out,
    accum_out,
    send_ref,
    table,
    half,
    scratch,
    sem,
):
    table_in = pltpu.make_async_copy(table_hbm, table, sem)
    table_in.start()
    named = named_rows(id_column(asks_ref, 2 * step + 2), table.shape[1])
    total = near_ref[...] + pair_gradient(mine_ref, far_low, far_high, table.shape[1])
    table_in.wait()
    accum_out[...] = adagrad(table, accum_ref[...], total[0:CUT, :], total[CUT:, :])
    table_done = pltpu.make_async_copy(table, table_out, sem)
    table_done.start()
    to_half(table, half, scratch)
    send_ref[...] = lookup(named, half)
    table_done.wait()


def word_final_body(
    mine_ref, far_low, far_high, near_ref, table_ref, accum_ref, table_out, accum_out
):
    width, words = table_ref.shape
    total = near_ref[...] + pair_gradient(mine_ref, far_low, far_high, words)
    grad = total[0:width, :]
    accum = accum_ref[...] + jnp.sum(grad * grad, axis=0, keepdims=True) * (1.0 / width)
    accum_out[...] = accum
    table_out[...] = table_ref[...] - grad * (LEARN * lax.rsqrt(accum))


def shape(*dims, dtype=F32):
    return jax.ShapeDtypeStruct(dims, dtype)


def exchange(x):
    return lax.all_to_all(x, "wide", split_axis=0, concat_axis=0, tiled=True)


def shifted(x, by):
    size = lax.axis_size("grp")
    return lax.ppermute(x, "grp", [(i, (i + by) % size) for i in range(size)])


def on_device(
    word_table,
    word_accum,
    ent_table,
    ent_accum,
    anchor_word_shard,
    anchor_word_row,
    anchor_ent_row,
    anchor_count,
    link_src_row,
    link_dst_shard,
    link_dst_row,
    link_count,
    neg_rows,
):
    peers = lax.axis_size("wide")
    message = peers * 2 * CAP
    word, ent = word_table.T, ent_table.T
    word_sum, ent_sum = word_accum[None, :], ent_accum[None, :]
    width, words = word.shape
    entities = ent.shape[1]
    indices = (
        anchor_word_shard[:, :, 0],
        link_dst_shard[:, :, 0],
        anchor_word_row,
        link_dst_row,
        anchor_ent_row,
        link_src_row,
        anchor_count.T,
        link_count.T,
    )
    asks, rows, cols = kernel_call(
        prepare_body,
        (shape(peers, BLOCK, dtype=jnp.int32), shape(STEPS * STRIDE, BLOCK), shape(BLOCK, BLOCK)),
        "prepare",
        indices,
        scratch=[pltpu.VMEM(x.shape, jnp.int32) for x in indices]
        + [pltpu.VMEM((BLOCK, BLOCK), F32), pltpu.SemaphoreType.DMA((len(indices),))],
        hbm=range(len(indices)),
        moved=2**18,
        pin=True,
    )
    asked = exchange(asks[:, None, :])[:, 0, :]
    half_shape = shape(PAD, entities, dtype=BF16)
    ent_half, word_half, pushed, counts, ent_sum, word_sum = kernel_call(
        halves_body,
        (
            half_shape,
            shape(PAD, words, dtype=BF16),
            shape(message, HALF, dtype=BF16),
            shape(8 * 2 * STEPS, entities),
            shape(1, entities),
            shape(1, words),
        ),
        "halves",
        (ent, word, neg_rows, ent_sum, word_sum, rows, cols),
        scratch=(
            pltpu.VMEM(ent.shape, F32),
            pltpu.VMEM(word.shape, F32),
            pltpu.VMEM(neg_rows.shape, jnp.int32),
            pltpu.VMEM((PAD, entities), F32),
            pltpu.SemaphoreType.DMA((5,)),
        ),
        hbm=range(5),
        moved=2**22,
        pin=True,
    )
    send_shape = shape(message, 3 * HALF, dtype=BF16)
    links_shape = shape(message, PAD, dtype=BF16)
    (send,) = kernel_call(
        respond_body,
        (send_shape,),
        "respond",
        (asked, pushed, word_half, ent_half),
        moved=2**22,
    )
    for step in range(STEPS):
        last = step == STEPS - 1
        recv = exchange(send)
        if step == 0:
            link_recv, link_at = recv, HALF
        (grads,) = kernel_call(
            functools.partial(anchor_body, step),
            (shape(message, HALF, dtype=BF16),),
            "anchor",
            (recv, rows, cols, counts, ent_half),
            moved=2**22,
        )
        received = exchange(grads)
        held = (pltpu.VMEM((width, entities), F32),)
        out = kernel_call(
            functools.partial(ent_update_body, step, last, link_at),
            (shape(width, entities), shape(1, entities)) + (() if last else (half_shape, links_shape)),
            "ent_update",
            (asked, rows, cols, counts, recv, link_recv, ent_half, ent, ent_sum),
            scratch=held
            + (
                ()
                if last
                else (pltpu.VMEM((PAD, entities), F32),)
            )
            + (pltpu.SemaphoreType.DMA((1,)),),
            hbm=(7,),
            hbm_out=(0,),
            moved=2**23,
        )
        ent, ent_sum = out[0], out[1]
        if not last:
            ent_half = out[2]
            received, links = lax.optimization_barrier((received, out[3]))
            link_recv, link_at = exchange(links), 0
        columns = (shape(CUT + HALF, peers * CAP, dtype=BF16),)
        columns += (shape(CUT + HALF, peers * CAP // 2, dtype=BF16),) * 4
        mine = kernel_call(compact_body, columns, "compact", (received,), moved=2**20)
        before_low, after_high = shifted(mine[1], 1), shifted(mine[4], -1)
        before_high, after_low = shifted(mine[2], 1), shifted(mine[3], -1)
        far_low, far_high = shifted(before_low, 1), shifted(after_high, -1)
        (near,) = kernel_call(
            word_near_body,
            (shape(CUT + HALF, words),),
            "word_near",
            (before_low, before_high, after_low, after_high),
            moved=2**21,
        )
        if last:
            word, word_sum = kernel_call(
                word_final_body,
                (shape(width, words), shape(1, words)),
                "word_final",
                (mine[0], far_low, far_high, near, word, word_sum),
                moved=2**23,
            )
        else:
            word, word_sum, send = kernel_call(
                functools.partial(word_update_body, step),
                (shape(width, words), shape(1, words), shape(message, HALF, dtype=BF16)),
                "word_update",
                (asked, mine[0], far_low, far_high, near, word, word_sum),
                scratch=(
                    pltpu.VMEM((width, words), F32),
                    pltpu.VMEM((PAD, words), BF16),
                    pltpu.VMEM((PAD, words), F32),
                    pltpu.SemaphoreType.DMA,
                ),
                hbm=(5,),
                hbm_out=(0,),
                moved=2**23,
            )
            send, link_recv = lax.optimization_barrier((send, link_recv))
    return (word.T, word_sum[0], ent.T, ent_sum[0])


def solution(mesh):
    in_specs = (
        P("wide", None),
        P("wide"),
        P(("grp", "wide"), None),
        P(("grp", "wide")),
        P(None, ("grp", "wide"), None),
        P(None, ("grp", "wide")),
        P(None, ("grp", "wide")),
        P(None, ("grp", "wide")),
        P(None, ("grp", "wide")),
        P(None, ("grp", "wide"), None),
        P(None, ("grp", "wide")),
        P(None, ("grp", "wide")),
        P(None, ("grp", "wide"), None),
    )
    out_specs = (P("wide", None), P("wide"), P(("grp", "wide"), None), P(("grp", "wide")))
    return jax.shard_map(
        on_device, mesh=mesh, in_specs=in_specs, out_specs=out_specs, check_vma=False
    )
```

```python
import functools

import jax
import jax.numpy as jnp
from jax import lax
from jax.experimental import pallas as pl
from jax.experimental.pallas import tpu as pltpu
from jax.sharding import PartitionSpec as P

BLOCK = 128
STEPS = 2
LEARN = 0.1
CAP = 4
HALF = 256
CUT = 248
PAD = 2 * HALF
ID_HI = 252
ID_LO = 253
F32 = jnp.float32
BF16 = jnp.bfloat16

PLACE_W, PLACE_L, RANK_W, RANK_L, WORD_ROW, LINK_ROW, ANCHOR_ENT, LINK_SRC, MASK_W, MASK_L = range(10)
STRIDE = 16


def iota(shape, dim):
    return lax.broadcasted_iota(jnp.int32, shape, dim).astype(F32)


def nn(a, b):
    return lax.dot_general(a, b, (((1,), (0,)), ((), ())), preferred_element_type=F32)


def nt(a, b):
    return lax.dot_general(a, b, (((1,), (1,)), ((), ())), preferred_element_type=F32)


def hot(condition):
    return jnp.where(condition, 1.0, 0.0).astype(BF16)


def split(x):
    high = x.astype(BF16)
    return high, (x - high.astype(F32)).astype(BF16)


def kernel_call(body, out_shape, name, operands, scratch=(), hbm=(), hbm_out=(), moved=0, pin=False):
    if pin:
        operands = [
            pltpu.with_memory_space_constraint(x, pltpu.HBM) if i in hbm else x
            for i, x in enumerate(operands)
        ]

    def space(far):
        return pl.BlockSpec(memory_space=pltpu.HBM if far else pltpu.VMEM)

    return pl.pallas_call(
        body,
        out_shape=out_shape,
        in_specs=[space(i in hbm) for i in range(len(operands))],
        out_specs=tuple(space(i in hbm_out) for i in range(len(out_shape))),
        scratch_shapes=list(scratch),
        name=name,
        compiler_params=pltpu.CompilerParams(vmem_limit_bytes=32 * 2**20),
        cost_estimate=pl.CostEstimate(flops=0, bytes_accessed=moved, transcendentals=0),
    )(*operands)


def fetch(sources, targets, sems):
    copies = [
        pltpu.make_async_copy(source, target, sems.at[i])
        for i, (source, target) in enumerate(zip(sources, targets))
    ]
    for copy in copies:
        copy.start()
    for copy in copies:
        copy.wait()


def prepare_body(*refs):
    sources, (asks_ref, rows_ref, cols_ref), (*held, table, sems) = refs[:8], refs[8:11], refs[11:]
    fetch(sources, held, sems)
    aws, lds, awr, ldr, aer, lsr, anchor_count, link_count = held
    peers = asks_ref.shape[0]
    table[...] = jnp.zeros_like(table)
    earlier = hot(iota((BLOCK, BLOCK), 0) < iota((BLOCK, BLOCK), 1))
    peer = iota((peers, BLOCK), 0)
    spot = iota((1, BLOCK), 1)

    def note(step, which, value):
        table[STRIDE * step + which : STRIDE * step + which + 1, :] = value

    kinds = [(step, kind) for step in range(STEPS) for kind in range(2)]
    shards = [(aws, lds)[kind][step : step + 1, :].astype(F32) for step, kind in kinds]
    owners = [peer == shard for shard in shards]
    owned = [hot(owner) for owner in owners]
    before = nn(jnp.concatenate(owned, axis=0), earlier)
    for i, (step, kind) in enumerate(kinds):
        counted = before[i * peers : (i + 1) * peers, :]
        rank = jnp.sum(jnp.where(owners[i], counted, 0.0), axis=0, keepdims=True)
        note(step, PLACE_W + kind, shards[i] * (2 * CAP) + rank)
        note(step, RANK_W + kind, rank)
        note(step, WORD_ROW + kind, (awr, ldr)[kind][step : step + 1, :].astype(F32))
        limit = (anchor_count, link_count)[kind][0:1, step : step + 1].astype(F32)
        note(step, MASK_W + kind, jnp.where(spot < limit, 1.0, 0.0))
    for step in range(STEPS):
        note(step, ANCHOR_ENT, aer[step : step + 1, :].astype(F32))
        note(step, LINK_SRC, lsr[step : step + 1, :].astype(F32))
    rows_ref[...] = table[0 : STEPS * STRIDE, :]
    cols = jnp.transpose(table[...])
    cols_ref[...] = cols
    lane = iota((BLOCK, BLOCK), 1)
    values = []
    for i, (step, kind) in enumerate(kinds):
        base = STRIDE * step + kind
        rank = cols[:, base + RANK_W : base + RANK_W + 1]
        row = cols[:, base + WORD_ROW : base + WORD_ROW + 1]
        high = jnp.floor(row * (1.0 / 16.0))
        place = i * CAP + rank
        value = jnp.where(
            lane == place, high, jnp.where(lane == place + 64.0, row - 16.0 * high, 0.0)
        )
        values.append(value.astype(BF16))
    asks = nn(jnp.concatenate(owned, axis=1), jnp.concatenate(values, axis=0))
    asks_ref[...] = asks.astype(jnp.int32)


def to_half(ref, out_ref, scratch):
    scratch[CUT:HALF, :] = jnp.zeros((HALF - CUT, scratch.shape[1]), F32)
    scratch[PAD - 8 : PAD, :] = jnp.zeros((8, scratch.shape[1]), F32)
    scratch[0:CUT, :] = ref[0:CUT, :]
    scratch[HALF : HALF + ref.shape[0] - CUT, :] = ref[CUT:, :]
    out_ref[...] = scratch[...].astype(BF16)


def halves_body(
    ent_hbm,
    word_hbm,
    neg_hbm,
    ent_sum_hbm,
    word_sum_hbm,
    rows_ref,
    cols_ref,
    ent_out,
    word_out,
    pushed_out,
    counts_out,
    ent_sum_out,
    word_sum_out,
    ent,
    word,
    neg,
    scratch,
    sems,
):
    copies = [
        pltpu.make_async_copy(source, target, sems.at[i])
        for i, (source, target) in enumerate(
            (
                (ent_hbm, ent),
                (word_hbm, word),
                (neg_hbm, neg),
                (ent_sum_hbm, ent_sum_out),
                (word_sum_hbm, word_sum_out),
            )
        )
    ]
    for copy in copies:
        copy.start()
    copies[0].wait()
    to_half(ent, ent_out, scratch)
    pushed_out[...] = pushed_sources(0, rows_ref, cols_ref, ent_out, pushed_out.shape[0])
    copies[1].wait()
    to_half(word, word_out, scratch)
    for copy in copies[2:]:
        copy.wait()
    entity = iota((ent.shape[1], neg.shape[-1]), 0)
    ones = jnp.ones((8, neg.shape[-1]), BF16)
    for i in range(2 * STEPS):
        named = hot(entity == neg[i // 2, i % 2 : i % 2 + 1, :].astype(F32))
        counts_out[8 * i : 8 * i + 8, :] = nt(ones, named)


def id_column(asks_ref, which):
    peers = asks_ref.shape[0]
    rows = peers * 2 * CAP
    source = hot(
        lax.broadcasted_iota(jnp.int32, (rows, peers), 0) // (2 * CAP)
        == lax.broadcasted_iota(jnp.int32, (rows, peers), 1)
    )
    spread = nn(source, asks_ref[...].astype(BF16))
    lane = lax.broadcasted_iota(jnp.int32, (rows, BLOCK), 1)
    place = which * CAP + lax.broadcasted_iota(jnp.int32, (rows, BLOCK), 0) % CAP
    weight = jnp.where(lane == place, 16.0, jnp.where(lane == place + 64, 1.0, 0.0))
    return jnp.sum(spread * weight, axis=1, keepdims=True)


def first_half(rows):
    return lax.broadcasted_iota(jnp.int32, (rows, HALF), 0) % (2 * CAP) < CAP


def named_rows(ids, count):
    return hot(iota((ids.shape[0], count), 1) == ids)


def lookup(named, half_ref):
    both = nt(named, half_ref[...])
    return jnp.where(first_half(named.shape[0]), both[:, 0:HALF], both[:, HALF:]).astype(BF16)


def column(cols_ref, step, which):
    return cols_ref[:, STRIDE * step + which : STRIDE * step + which + 1]


def row_of(rows_ref, step, which):
    return rows_ref[STRIDE * step + which : STRIDE * step + which + 1, :]


def sigmoid(x):
    return jax.nn.sigmoid(x)


def product(coef, half_ref):
    high, low = split(coef)
    both = nt(jnp.concatenate([high, low], axis=0), half_ref[...])
    return both[0 : coef.shape[0], :] + both[coef.shape[0] :, :]


def sources(step, cols_ref, ent_half):
    named = hot(iota((BLOCK, ent_half.shape[1]), 1) == column(cols_ref, step, LINK_SRC))
    return named, nt(named, ent_half[...]).astype(BF16)


def pushed_sources(step, rows_ref, cols_ref, ent_half, rows):
    place = jnp.where(
        row_of(rows_ref, step, MASK_L) > 0.0, row_of(rows_ref, step, PLACE_L), -float(2 * CAP)
    )
    _, src = sources(step, cols_ref, ent_half)
    return put(place, src[:, 0:HALF], src[:, HALF:PAD], rows).astype(BF16)


def asked_rows(which, asks_ref, half_ref):
    return lookup(named_rows(id_column(asks_ref, which), half_ref.shape[1]), half_ref)


def respond_body(asks_ref, pushed_ref, word_half, ent_half, out_ref):
    out_ref[:, 0:HALF] = asked_rows(0, asks_ref, word_half)
    out_ref[:, HALF:PAD] = asked_rows(1, asks_ref, ent_half)
    out_ref[:, PAD:] = pushed_ref[...]


def take(recv, place):
    rows = recv.shape[0]
    lane = iota((2 * BLOCK, rows), 1)
    named = hot(lane == jnp.concatenate([place, place + CAP], axis=0))
    both = nn(named, recv)
    return jnp.concatenate([both[0:BLOCK, :], both[BLOCK:, :]], axis=1)


def put(place, low, high, rows):
    row = iota((rows, 2 * BLOCK), 0)
    named = hot(row == jnp.concatenate([place, place + CAP], axis=1))
    return nn(named, jnp.concatenate([low, high], axis=0))


def anchor_coefficients(step, words, cols_ref, counts_ref, ent_half):
    mask = column(cols_ref, step, MASK_W)
    score = nn(words, ent_half[...])
    target = iota(score.shape, 1) == column(cols_ref, step, ANCHOR_ENT)
    pos = jnp.sum(jnp.where(target, score, 0.0), axis=1, keepdims=True)
    pull = mask * (sigmoid(pos) - 1.0)
    push = (mask * sigmoid(score)).astype(BF16).astype(F32)
    return push * counts_ref[16 * step : 16 * step + 1, :] + jnp.where(target, pull, 0.0)


def anchor_body(step, recv_ref, rows_ref, cols_ref, counts_ref, ent_half, send_ref):
    words = take(recv_ref[:, 0:HALF], column(cols_ref, step, PLACE_W)).astype(BF16)
    centre = product(anchor_coefficients(step, words, cols_ref, counts_ref, ent_half), ent_half)
    word_row = column(cols_ref, step, WORD_ROW)
    id_high = jnp.floor(word_row * (1.0 / 16.0))
    lane = lax.broadcasted_iota(jnp.int32, (BLOCK, PAD), 1) % HALF
    centre = jnp.where(
        lane == ID_HI, id_high, jnp.where(lane == ID_LO, word_row - 16.0 * id_high, centre)
    ).astype(BF16)
    place = row_of(rows_ref, step, PLACE_W)
    send_ref[...] = put(place, centre[:, 0:HALF], centre[:, HALF:PAD], send_ref.shape[0]).astype(BF16)


def adagrad(table_ref, accum, low, high):
    width = table_ref.shape[0]
    low = low[0:CUT, :]
    high = high[0 : width - CUT, :]
    square = jnp.sum(low * low, axis=0, keepdims=True) + jnp.sum(high * high, axis=0, keepdims=True)
    accum = accum + square * (1.0 / width)
    rate = LEARN * lax.rsqrt(accum)
    table_ref[0:CUT, :] = table_ref[0:CUT, :] - low * rate
    table_ref[CUT:, :] = table_ref[CUT:, :] - high * rate
    return accum


def ent_update_body(
    step,
    last,
    link_at,
    asks_ref,
    rows_ref,
    cols_ref,
    counts_ref,
    recv_ref,
    link_recv,
    ent_half,
    table_hbm,
    accum_ref,
    table_out,
    accum_out,
    *rest,
):
    if last:
        table, sems = rest
    else:
        half_out, links_out, table, scratch, sems = rest
    rows = recv_ref.shape[0]
    table_in = pltpu.make_async_copy(table_hbm, table, sems.at[0])
    table_in.start()
    words = take(recv_ref[:, 0:HALF], column(cols_ref, step, PLACE_W)).astype(BF16)
    coef = anchor_coefficients(step, words, cols_ref, counts_ref, ent_half)
    source, src = sources(step, cols_ref, ent_half)
    mask = column(cols_ref, step, MASK_L)
    push = (mask * sigmoid(nn(src, ent_half[...]))).astype(BF16).astype(F32)
    link_coef = push * counts_ref[16 * step + 8 : 16 * step + 9, :]
    targets = take(link_recv[:, link_at : link_at + HALF], column(cols_ref, step, PLACE_L))
    src_float = src.astype(F32)
    pos = jnp.sum(src_float * targets, axis=1, keepdims=True)
    pull = mask * (sigmoid(pos) - 1.0)
    link_grad = pull * targets + product(link_coef, ent_half)
    centres = jnp.concatenate([words.astype(F32), src_float], axis=0)
    centres = jnp.transpose(centres).astype(BF16)
    high, low = split(jnp.concatenate([coef, link_coef], axis=0))
    total = nn(centres, high) + nn(centres, low)
    high, low = split(jnp.transpose(link_grad))
    total = total + nn(high, source) + nn(low, source)
    named = named_rows(id_column(asks_ref, 2 * step + 1), ent_half.shape[1])
    pushed = jnp.transpose(link_recv[:, link_at + HALF :].astype(F32))
    lower = lax.broadcasted_iota(jnp.int32, (1, rows), 1) % (2 * CAP) < CAP
    held = jnp.where(lower, nt(ent_half[0:HALF, :], named), nt(ent_half[HALF:PAD, :], named))
    part = jnp.sum(pushed * held, axis=0, keepdims=True)
    other = jnp.where(lower, jnp.roll(part, -CAP, axis=1), jnp.roll(part, CAP, axis=1))
    grads = (sigmoid(part + other) - 1.0) * pushed
    low = nn(jnp.where(lower, grads, 0.0).astype(BF16), named) + total[0:HALF, :]
    high = nn(jnp.where(lower, 0.0, grads).astype(BF16), named) + total[HALF:PAD, :]
    table_in.wait()
    accum_out[...] = adagrad(table, accum_ref[...], low, high)
    table_done = pltpu.make_async_copy(table, table_out, sems.at[0])
    table_done.start()
    if not last:
        to_half(table, half_out, scratch)
        links_out[:, 0:HALF] = asked_rows(2 * step + 3, asks_ref, half_out)
        links_out[:, HALF:] = pushed_sources(step + 1, rows_ref, cols_ref, half_out, rows)
    table_done.wait()


def compact_body(recv_ref, *outs):
    rows = recv_ref.shape[0]
    places = outs[0].shape[1]
    grads = jnp.transpose(recv_ref[...].astype(F32)).astype(BF16)
    row = lax.broadcasted_iota(jnp.int32, (rows, places), 0)
    place = lax.broadcasted_iota(jnp.int32, (rows, places), 1)
    place = place // CAP * (2 * CAP) + place % CAP
    low = nn(grads, hot(row == place))
    high = nn(grads, hot(row == place + CAP))
    columns = jnp.concatenate([low[0:CUT, :], high], axis=0).astype(BF16)
    outs[0][...] = columns
    for i, out in enumerate(outs[1:]):
        half = out.shape[1]
        out[...] = columns[:, i % 2 * half : (i % 2 + 1) * half]


def word_gradient(columns, count):
    depth, places = columns.shape
    ids = columns[depth - 8 :, :].astype(F32)
    ids = ids[4:5, :] * 16.0 + ids[5:6, :]
    return nt(columns, hot(iota((count, places), 0) == ids))


def joined(first_ref, second_ref):
    return jnp.concatenate([first_ref[...], second_ref[...]], axis=1)


def pair_gradient(mine_ref, far_low, far_high, count):
    mine = word_gradient(mine_ref[...], count)
    return mine + word_gradient(joined(far_low, far_high), count)


def word_near_body(before_low, before_high, after_low, after_high, out_ref):
    count = out_ref.shape[1]
    before = word_gradient(joined(before_low, before_high), count)
    out_ref[...] = before + word_gradient(joined(after_low, after_high), count)


def word_update_body(
    step,
    asks_ref,
    mine_ref,
    far_low,
    far_high,
    near_ref,
    table_hbm,
    accum_ref,
    table_out,
    accum_out,
    send_ref,
    table,
    half,
    scratch,
    sem,
):
    table_in = pltpu.make_async_copy(table_hbm, table, sem)
    table_in.start()
    named = named_rows(id_column(asks_ref, 2 * step + 2), table.shape[1])
    total = near_ref[...] + pair_gradient(mine_ref, far_low, far_high, table.shape[1])
    table_in.wait()
    accum_out[...] = adagrad(table, accum_ref[...], total[0:CUT, :], total[CUT:, :])
    table_done = pltpu.make_async_copy(table, table_out, sem)
    table_done.start()
    to_half(table, half, scratch)
    send_ref[...] = lookup(named, half)
    table_done.wait()


def word_final_body(
    mine_ref, far_low, far_high, near_ref, table_ref, accum_ref, table_out, accum_out, table, sems
):
    width, words = table_ref.shape
    total = near_ref[...] + pair_gradient(mine_ref, far_low, far_high, words)
    grad = total[0:width, :]
    accum = accum_ref[...] + jnp.sum(grad * grad, axis=0, keepdims=True) * (1.0 / width)
    accum_out[...] = accum
    rate = LEARN * lax.rsqrt(accum)
    copies = []
    for i, (start, end) in enumerate(((0, HALF), (HALF, width))):
        table[start:end, :] = table_ref[start:end, :] - grad[start:end, :] * rate
        copies.append(
            pltpu.make_async_copy(table.at[start:end], table_out.at[start:end], sems.at[i])
        )
        copies[i].start()
    for copy in copies:
        copy.wait()


def shape(*dims, dtype=F32):
    return jax.ShapeDtypeStruct(dims, dtype)


def exchange(x):
    return lax.all_to_all(x, "wide", split_axis=0, concat_axis=0, tiled=True)


def shifted(x, by):
    size = lax.axis_size("grp")
    return lax.ppermute(x, "grp", [(i, (i + by) % size) for i in range(size)])


def on_device(
    word_table,
    word_accum,
    ent_table,
    ent_accum,
    anchor_word_shard,
    anchor_word_row,
    anchor_ent_row,
    anchor_count,
    link_src_row,
    link_dst_shard,
    link_dst_row,
    link_count,
    neg_rows,
):
    peers = lax.axis_size("wide")
    message = peers * 2 * CAP
    word, ent = word_table.T, ent_table.T
    word_sum, ent_sum = word_accum[None, :], ent_accum[None, :]
    width, words = word.shape
    entities = ent.shape[1]
    indices = (
        anchor_word_shard[:, :, 0],
        link_dst_shard[:, :, 0],
        anchor_word_row,
        link_dst_row,
        anchor_ent_row,
        link_src_row,
        anchor_count.T,
        link_count.T,
    )
    asks, rows, cols = kernel_call(
        prepare_body,
        (shape(peers, BLOCK, dtype=jnp.int32), shape(STEPS * STRIDE, BLOCK), shape(BLOCK, BLOCK)),
        "prepare",
        indices,
        scratch=[pltpu.VMEM(x.shape, jnp.int32) for x in indices]
        + [pltpu.VMEM((BLOCK, BLOCK), F32), pltpu.SemaphoreType.DMA((len(indices),))],
        hbm=range(len(indices)),
        moved=2**18,
        pin=True,
    )
    asked = exchange(asks[:, None, :])[:, 0, :]
    half_shape = shape(PAD, entities, dtype=BF16)
    ent_half, word_half, pushed, counts, ent_sum, word_sum = kernel_call(
        halves_body,
        (
            half_shape,
            shape(PAD, words, dtype=BF16),
            shape(message, HALF, dtype=BF16),
            shape(8 * 2 * STEPS, entities),
            shape(1, entities),
            shape(1, words),
        ),
        "halves",
        (ent, word, neg_rows, ent_sum, word_sum, rows, cols),
        scratch=(
            pltpu.VMEM(ent.shape, F32),
            pltpu.VMEM(word.shape, F32),
            pltpu.VMEM(neg_rows.shape, jnp.int32),
            pltpu.VMEM((PAD, entities), F32),
            pltpu.SemaphoreType.DMA((5,)),
        ),
        hbm=range(5),
        moved=2**22,
        pin=True,
    )
    send_shape = shape(message, 3 * HALF, dtype=BF16)
    links_shape = shape(message, PAD, dtype=BF16)
    (send,) = kernel_call(
        respond_body,
        (send_shape,),
        "respond",
        (asked, pushed, word_half, ent_half),
        moved=2**22,
    )
    for step in range(STEPS):
        last = step == STEPS - 1
        recv = exchange(send)
        if step == 0:
            link_recv, link_at = recv, HALF
        (grads,) = kernel_call(
            functools.partial(anchor_body, step),
            (shape(message, HALF, dtype=BF16),),
            "anchor",
            (recv, rows, cols, counts, ent_half),
            moved=2**22,
        )
        received = exchange(grads)
        held = (pltpu.VMEM((width, entities), F32),)
        out = kernel_call(
            functools.partial(ent_update_body, step, last, link_at),
            (shape(width, entities), shape(1, entities)) + (() if last else (half_shape, links_shape)),
            "ent_update",
            (asked, rows, cols, counts, recv, link_recv, ent_half, ent, ent_sum),
            scratch=held
            + (
                ()
                if last
                else (pltpu.VMEM((PAD, entities), F32),)
            )
            + (pltpu.SemaphoreType.DMA((1,)),),
            hbm=(7,),
            hbm_out=(0,),
            moved=2**23,
        )
        ent, ent_sum = out[0], out[1]
        if not last:
            ent_half = out[2]
            received, links = lax.optimization_barrier((received, out[3]))
            link_recv, link_at = exchange(links), 0
        columns = (shape(CUT + HALF, peers * CAP, dtype=BF16),)
        columns += (shape(CUT + HALF, peers * CAP // 2, dtype=BF16),) * 4
        mine = kernel_call(compact_body, columns, "compact", (received,), moved=2**20)
        before_low, after_high = shifted(mine[1], 1), shifted(mine[4], -1)
        before_high, after_low = shifted(mine[2], 1), shifted(mine[3], -1)
        far_low, far_high = shifted(before_low, 1), shifted(after_high, -1)
        (near,) = kernel_call(
            word_near_body,
            (shape(CUT + HALF, words),),
            "word_near",
            (before_low, before_high, after_low, after_high),
            moved=2**21,
        )
        if last:
            word, word_sum = kernel_call(
                word_final_body,
                (shape(width, words), shape(1, words)),
                "word_final",
                (mine[0], far_low, far_high, near, word, word_sum),
                scratch=(pltpu.VMEM((width, words), F32), pltpu.SemaphoreType.DMA((2,))),
                hbm_out=(0,),
                moved=2**23,
            )
        else:
            word, word_sum, send = kernel_call(
                functools.partial(word_update_body, step),
                (shape(width, words), shape(1, words), shape(message, HALF, dtype=BF16)),
                "word_update",
                (asked, mine[0], far_low, far_high, near, word, word_sum),
                scratch=(
                    pltpu.VMEM((width, words), F32),
                    pltpu.VMEM((PAD, words), BF16),
                    pltpu.VMEM((PAD, words), F32),
                    pltpu.SemaphoreType.DMA,
                ),
                hbm=(5,),
                hbm_out=(0,),
                moved=2**23,
            )
            send, link_recv = lax.optimization_barrier((send, link_recv))
    return (word.T, word_sum[0], ent.T, ent_sum[0])


def solution(mesh):
    in_specs = (
        P("wide", None),
        P("wide"),
        P(("grp", "wide"), None),
        P(("grp", "wide")),
        P(None, ("grp", "wide"), None),
        P(None, ("grp", "wide")),
        P(None, ("grp", "wide")),
        P(None, ("grp", "wide")),
        P(None, ("grp", "wide")),
        P(None, ("grp", "wide"), None),
        P(None, ("grp", "wide")),
        P(None, ("grp", "wide")),
        P(None, ("grp", "wide"), None),
    )
    out_specs = (P("wide", None), P("wide"), P(("grp", "wide"), None), P(("grp", "wide")))
    return jax.shard_map(
        on_device, mesh=mesh, in_specs=in_specs, out_specs=out_specs, check_vma=False
    )
```
